512 devices in a mesh: expert: 32 (over x, y), tensor: 16 (over z, core).
Axes of the slice: x: 4, y: 8, z: 8, core: 2. Of those that a mesh axis runs over, the one named last changes fastest.
Arguments:
- hidden: bfloat16 [160, 131072], P(None, ('expert', 'tensor')), may hold values from -6 to 6
- codes: bfloat16 [131072, 6144], P(('expert', 'tensor')), may hold values from -8 to 7, as said below
- scales: float32 [2048, 6144], P(('expert', 'tensor')), may hold values from 0.001 to 0.004
- signs: int32 [131072], P(('expert', 'tensor')), may hold values from 0 to 1
- lowrank_down_map: bfloat16 [131072, 64], P(('expert', 'tensor')), may hold values from -0.046875 to 0.046875
- lowrank_up_map: bfloat16 [8, 64, 6144], P(None, None, 'tensor'), may hold values from -0.75 to 0.75
- experts: int32 [512, 2], P('expert'), may hold values from 0 to 7, all different within a row; in each aligned block of 16 rows (0 to 15, 16 to 31, ...) at most 5 rows name the same one
- gates: float32 [512, 2], P('expert'), may hold values from 0.2 to 1
- output_gradient: bfloat16 [512, 6144], P('expert', 'tensor'), may hold values from -6 to 6
Outputs:
- mixed: bfloat16 [512, 6144], P('expert', 'tensor')
- hidden_gradient: bfloat16 [160, 131072], P(None, ('expert', 'tensor'))
- down_map_gradient: float32 [131072, 64], P(('expert', 'tensor'))
- up_map_gradient: float32 [8, 64, 6144], P(None, None, 'tensor')
- gates_gradient: float32 [512, 2], P('expert')
The draws below stay inside these ranges and needn't reach their ends.
Inputs may be any that keep to these rules, and one draw needn't show every extreme that they name: The two experts of a token differ; among the 16 tokens of one index of the expert axis no expert is named more than 5 times, a bound that some block reaches. `codes`: whole numbers.
All inputs are finite; a program needn't handle non-finite values.
Results may differ from the reference program's by a relative error of at most 0.0056.
Values may be sent and summed in bfloat16 or wider, within the bound.
No kernel may reach another device: no remote copies, remote signals or barrier semaphores. Data moves between devices by JAX's collectives and lax.ppermute only.
A program may use at most 64 MiB of HBM per device.

```python
import math
import jax
import jax.numpy as jnp
import numpy as np
from jax import lax

MODEL_WIDTH = 6144
HIDDEN_UNITS = 16384
EXPERT_COUNT = 8
ADAPTER_RANK = 64
GROUP = 64
TOK_DEV = 16
CAP = 5
SLOTS = 160
TOKENS = 512
N_EXPERT = 32
N_TENSOR = 16


def draw_codes(key, part):
    key = jax.random.fold_in(key, 7)
    levels = jax.random.randint(key, (EXPERT_COUNT * HIDDEN_UNITS, MODEL_WIDTH), -8, 8, dtype=jnp.int32)
    return levels.astype(jnp.bfloat16)


def place_ends(values, own_key, least, top_value):
    spot = [jax.random.randint(jax.random.fold_in(own_key, axis), (), 0, length) for axis, length in enumerate(values.shape)]
    longest = values.shape.index(max(values.shape))
    neighbour = spot[:longest] + [(spot[longest] + 1) % values.shape[longest]] + spot[longest + 1:]
    return values.at[tuple(spot)].set(least).at[tuple(neighbour)].set(top_value)


def level_of(rng, dims, pieces, least, top_value):
    def one(position, blocks):
        draws = jax.random.uniform(jax.random.fold_in(jax.random.fold_in(rng, 6), position), (blocks,), jnp.float32, least / len(pieces), top_value / len(pieces))
        return jnp.repeat(jnp.exp(draws), dims[position] // blocks).reshape((-1,) + (1,) * (len(dims) - position - 1))

    factor_of = one(*pieces[0])
    for cut in pieces[1:]:
        factor_of = factor_of * one(*cut)
    return factor_of


def assign_block(stream_key, own, number, rows, number_of, top, bound, lean):
    sequence = jax.random.permutation(stream_key, number_of)
    heavy_load, common = portions_of(number_of, rows * top, bound, lean, True), portions_of(number_of, rows * top, bound, lean, False)
    places = jnp.arange(number_of)

    def named(lengths, rotation):
        used = int((lengths > 0).sum())
        fixed = max(1, used // 4)
        shifted = fixed + (places - fixed + rotation * (used - fixed)) % max(1, number_of - fixed)
        return jnp.zeros((number_of,), jnp.int32).at[sequence[jnp.where(places < fixed, places, shifted)]].set(jnp.asarray(lengths, jnp.int32))

    lengths = jnp.where(number % 4 == 0, named(heavy_load, number // 4), named(common, number - number // 4 - 1))
    mixed = jax.random.permutation(jax.random.fold_in(own, 3), number_of)
    donor, receiver = mixed[0:number_of // 2 * 2:2], mixed[1:number_of // 2 * 2:2]
    margin = jnp.minimum(lengths[donor] - 1, bound - lengths[receiver]) // 2
    margin = jnp.where((donor == sequence[0]) | (receiver == sequence[0]) | (lengths[receiver] == 0), 0, jnp.maximum(margin, 0))
    shifted = jax.random.randint(jax.random.fold_in(own, 4), (number_of // 2,), 0, 1 << 20) % (margin + 1)
    lengths = lengths.at[donor].add(-shifted).at[receiver].add(shifted)
    labels = jnp.searchsorted(jnp.cumsum(lengths), jnp.arange(rows * top), side="right").astype(jnp.int32)
    table = labels.reshape(top, rows).T
    table = table[jax.random.permutation(jax.random.fold_in(own, 1), rows)]
    rotation = jax.random.randint(jax.random.fold_in(own, 2), (rows, 1), 0, top)
    return jnp.take_along_axis(table, (jnp.arange(top)[None, :] + rotation) % top, axis=1)


def portions_of(number_of, total, reach, slope, full):
    weights = [(1 << 20) // math.isqrt(standing ** slope) + 1 for standing in range(1, number_of + 1)]
    largest = reach if full else min(reach, max(-(-total // number_of), total * weights[0] // sum(weights)))
    least = 1 if total - largest >= number_of - 1 else 0
    holding, surplus = [largest] + [least] * (number_of - 1), total - largest - least * (number_of - 1)
    while surplus > 0:
        movable = [i for i in range(1, number_of) if holding[i] < largest] or [i for i in range(1, number_of) if holding[i] < reach]
        whole, remaining = sum([weights[i] for i in movable]), surplus
        for i in movable:
            more = min(reach - holding[i], max(1, remaining * weights[i] // whole), surplus)
            holding[i] = holding[i] + more
            surplus = surplus - more
    return np.array(holding)


def normal_values(own_key, shape, deviation, reach, shards=(), kind=jnp.bfloat16):
    drawn = deviation * jax.random.normal(own_key, shape, jnp.float32)
    if shards:
        drawn = drawn * level_of(own_key, shape, shards, -0.22, 0.18)
    return jnp.clip(drawn, -reach, reach).astype(kind)


def setup_inputs(seed: int = 0) -> dict:
    key_of = jax.random.split(jax.random.key(seed), 10)
    hidden = normal_values(key_of[0], (SLOTS, EXPERT_COUNT * HIDDEN_UNITS), 1.0, 6.0, ((1, 512),))
    codes = draw_codes(jax.random.fold_in(key_of[9], 71), 0)
    scales = jnp.clip(jnp.exp(math.log(0.004) - 1.3862944 * jax.random.uniform(key_of[2], (EXPERT_COUNT * HIDDEN_UNITS // GROUP, MODEL_WIDTH), jnp.float32) ** level_of(key_of[2], (EXPERT_COUNT * HIDDEN_UNITS // GROUP, MODEL_WIDTH), ((0, 512),), -0.2, 0.2)), 0.001, 0.004)
    signs = place_ends(jax.random.randint(key_of[3], (EXPERT_COUNT * HIDDEN_UNITS,), 0, 2), jax.random.fold_in(key_of[3], 1), 0, 1).astype(jnp.int32)
    lowrank_down_map = normal_values(key_of[4], (EXPERT_COUNT * HIDDEN_UNITS, ADAPTER_RANK), HIDDEN_UNITS ** -0.5, 0.046875, ((0, 512),))
    lowrank_up_map = normal_values(key_of[5], (EXPERT_COUNT, ADAPTER_RANK, MODEL_WIDTH), ADAPTER_RANK ** -0.5, 0.75, ((2, 16),))
    experts_keys = jax.random.split(jax.random.fold_in(key_of[6], 1), TOKENS // TOK_DEV)
    experts_turns = jax.random.permutation(jax.random.fold_in(key_of[6], 3), TOKENS // TOK_DEV)
    experts = jax.vmap(lambda own, number: assign_block(jax.random.fold_in(key_of[6], 2), own, number, TOK_DEV, EXPERT_COUNT, 2, CAP, 2))(experts_keys, experts_turns).reshape((TOKENS, 2))
    gates = jnp.clip(0.2 + 0.8 * jax.random.uniform(key_of[7], (TOKENS, 2), jnp.float32) ** level_of(key_of[7], (TOKENS, 2), ((0, 32),), -0.2, 0.2), 0.2, 1.0)
    output_gradient = normal_values(key_of[8], (TOKENS, MODEL_WIDTH), 1.0, 6.0, ((0, 32), (1, 16)))
    return {"hidden": hidden, "codes": codes, "scales": scales, "signs": signs, "lowrank_down_map": lowrank_down_map, "lowrank_up_map": lowrank_up_map, "experts": experts, "gates": gates, "output_gradient": output_gradient}


LOWRANK_SCALE = 0.5
HIGH_ACCURACY = lax.Precision.HIGHEST

def sylvester(count):
    table = np.ones((1, 1), np.float32)
    while table.shape[0] < count:
        table = np.kron(np.array([[1.0, 1.0], [1.0, -1.0]], np.float32), table)
    return jnp.asarray(table)

def rotate_full(values, blocks):
    height = values.shape[0]
    stride = values.shape[1] // blocks
    shaped = values.reshape(height, blocks, stride)
    shaped = jnp.einsum('sbj,jk->sbk', shaped, sylvester(stride), precision=HIGH_ACCURACY)
    shaped = jnp.einsum('cb,sbj->scj', sylvester(blocks), shaped, precision=HIGH_ACCURACY)
    return shaped.reshape(height, blocks * stride)

def reference(hidden, codes, scales, signs, lowrank_down_map, lowrank_up_map, experts, gates, output_gradient):
    replicas = N_EXPERT // EXPERT_COUNT
    blocks = replicas * N_TENSOR
    scaling = 1.0 / math.sqrt(HIDDEN_UNITS)
    flat_ids = experts.reshape(N_EXPERT, TOK_DEV * 2)
    assigned = (flat_ids[:, :, None] == jnp.arange(EXPERT_COUNT, dtype=jnp.int32)[None, None, :]).astype(jnp.int32)
    earlier = jnp.cumsum(assigned, axis=1) - assigned
    slot = lax.optimization_barrier(jnp.sum(earlier * assigned, axis=2))
    source = jnp.arange(N_EXPERT, dtype=jnp.int32)[:, None]
    target = (flat_ids * SLOTS + source * CAP + slot).reshape(TOKENS * 2).astype(jnp.int32)
    grad_values = output_gradient.astype(jnp.float32)
    weighted = (gates[:, :, None] * grad_values[:, None, :]).reshape(TOKENS * 2, MODEL_WIDTH)
    d_slots_all = jnp.zeros((EXPERT_COUNT * SLOTS, MODEL_WIDTH), jnp.float32).at[target].add(weighted).astype(jnp.bfloat16)
    slot_list = []
    hidden_list = []
    down_map_list = []
    up_map_list = []
    for expert_number in range(EXPERT_COUNT):
        low_projection = expert_number * HIDDEN_UNITS
        sign_values = (2 * signs[low_projection:low_projection + HIDDEN_UNITS] - 1).astype(jnp.float32)
        rotated_hidden = (rotate_full(hidden[:, low_projection:low_projection + HIDDEN_UNITS].astype(jnp.float32) * sign_values, blocks) * scaling).astype(jnp.bfloat16)
        group_scales = jnp.repeat(scales[low_projection // GROUP:(low_projection + HIDDEN_UNITS) // GROUP], GROUP, axis=0)
        weights = (codes[low_projection:low_projection + HIDDEN_UNITS].astype(jnp.float32) * group_scales).astype(jnp.bfloat16)
        lowrank_down = lowrank_down_map[low_projection:low_projection + HIDDEN_UNITS]
        lowrank_input = jnp.dot(rotated_hidden, lowrank_down, preferred_element_type=jnp.float32)
        frozen_output = jnp.dot(rotated_hidden, weights, preferred_element_type=jnp.float32)
        slot_output = frozen_output + LOWRANK_SCALE * jnp.dot(lowrank_input, lowrank_up_map[expert_number].astype(jnp.float32), precision=HIGH_ACCURACY)
        slot_list.append(slot_output)
        slot_gradient = d_slots_all[expert_number * SLOTS:(expert_number + 1) * SLOTS]
        lowrank_gradient = LOWRANK_SCALE * jnp.dot(slot_gradient, lowrank_up_map[expert_number].T, preferred_element_type=jnp.float32)
        up_map_list.append(LOWRANK_SCALE * jnp.dot(lowrank_input.T, slot_gradient.astype(jnp.float32), precision=HIGH_ACCURACY))
        rotated_gradient = jnp.dot(slot_gradient, weights.T, preferred_element_type=jnp.float32)
        rotated_gradient = rotated_gradient + jnp.dot(lowrank_gradient, lowrank_down.astype(jnp.float32).T, precision=HIGH_ACCURACY)
        down_map_list.append(jnp.dot(rotated_hidden.astype(jnp.float32).T, lowrank_gradient, precision=HIGH_ACCURACY))
        hidden_list.append((rotate_full(rotated_gradient, blocks) * scaling * sign_values).astype(jnp.bfloat16))
    slot_all = jnp.concatenate(slot_list, axis=0)
    picked = slot_all[target].reshape(TOKENS, 2, MODEL_WIDTH)
    mixed = lax.optimization_barrier(jnp.sum(gates[:, :, None] * picked, axis=1)).astype(jnp.bfloat16)
    gates_gradient = lax.optimization_barrier(jnp.sum(grad_values[:, None, :] * picked, axis=2))
    hidden_gradient = jnp.concatenate(hidden_list, axis=1)
    down_map_gradient = jnp.concatenate(down_map_list, axis=0)
    up_map_gradient = jnp.stack(up_map_list, axis=0)
    return (mixed, hidden_gradient, down_map_gradient, up_map_gradient, gates_gradient)
```

```python
import math

import jax
import jax.numpy as jnp
import numpy as np
from jax import lax
from jax.sharding import Mesh
from jax.sharding import PartitionSpec as P

HIDDEN_UNITS = 16384
EXPERT_COUNT = 8
LOWRANK_SCALE = 0.5
HIGH_ACCURACY = lax.Precision.HIGHEST
BF = jnp.bfloat16
F32 = jnp.float32
EXPERT = ("e", "r")
TENSOR = ("z", "c")
SLAB = ("r", "z", "c")
LANES = 128


def sylvester(count):
    table = np.ones((1, 1), np.float32)
    while table.shape[0] < count:
        table = np.kron(np.array([[1.0, 1.0], [1.0, -1.0]], np.float32), table)
    return jnp.asarray(table, BF)


def exchange(value, axes):
    return lax.all_to_all(value, axes, split_axis=0, concat_axis=0, tiled=True)


def to_chunks(values, peers):
    height, stride = values.shape
    halves = stride // LANES
    blocks = peers // halves
    shaped = values.reshape(blocks, height // blocks, halves, LANES)
    return shaped.transpose(0, 2, 1, 3).reshape(peers, height // blocks, LANES)


def from_chunks(chunks, height, stride):
    halves = stride // LANES
    blocks = chunks.shape[0] // halves
    shaped = chunks.reshape(blocks, halves, height // blocks, LANES)
    return shaped.transpose(0, 2, 1, 3).reshape(height, stride)


def mix_blocks(chunks):
    peers, rows, lanes = chunks.shape
    mixed = jnp.dot(
        sylvester(peers), chunks.reshape(peers, rows * lanes), preferred_element_type=F32
    )
    return mixed.astype(BF).reshape(peers, rows, lanes)


def body(
    hidden, codes, scales, signs, lowrank_down_map, lowrank_up_map, experts, gates, output_gradient
):
    slot_rows, stride = hidden.shape
    replicas, depth, cores = lax.axis_size("r"), lax.axis_size("z"), lax.axis_size("c")
    devices = EXPERT_COUNT * replicas
    peers = replicas * depth * cores
    rank = lowrank_down_map.shape[1]
    expert_position = lax.axis_index("e")
    replica = lax.axis_index("r")
    core = lax.axis_index("c")
    capacity = slot_rows // devices
    tokens_here = experts.shape[0]
    columns = output_gradient.shape[1]
    scaling = 1.0 / math.sqrt(HIDDEN_UNITS)
    sign_values = (2 * signs - 1).astype(F32)
    group_size = codes.shape[0] // scales.shape[0]

    flat_ids = experts.reshape(tokens_here * 2)
    assigned = (flat_ids[:, None] == jnp.arange(EXPERT_COUNT, dtype=jnp.int32)[None, :]).astype(
        jnp.int32
    )
    earlier = jnp.cumsum(assigned, axis=0) - assigned
    slot_index = jnp.sum(earlier * assigned, axis=1)
    target = flat_ids * capacity + slot_index
    row = jnp.arange(devices * capacity, dtype=jnp.int32)
    row_slot = row // (replicas * capacity) * capacity + row % capacity
    copier = (row_slot[:, None] == target[None, :]).astype(BF)
    weighted = (
        (gates[:, :, None] * output_gradient.astype(F32)[:, None, :])
        .reshape(tokens_here * 2, columns)
        .astype(BF)
    )
    outgoing = jnp.dot(copier, weighted, preferred_element_type=F32).astype(BF)
    d_rows = exchange(outgoing, EXPERT)
    lowrank_local = lax.dynamic_index_in_dim(lowrank_up_map, expert_position, 0, keepdims=False)
    gathered = lax.all_gather(
        jnp.concatenate([d_rows, lowrank_local], axis=0), TENSOR, axis=1, tiled=True
    )

    signed = (hidden.astype(F32) * sign_values).astype(BF)
    mixed_blocks = mix_blocks(exchange(to_chunks(signed, peers), SLAB))
    unrotated = from_chunks(exchange(mixed_blocks, SLAB), slot_rows, stride)
    spread_local = sylvester(stride)
    rotated = (jnp.dot(unrotated, spread_local, preferred_element_type=F32) * scaling).astype(BF)

    weights = (codes.astype(F32) * jnp.repeat(scales, group_size, axis=0)).astype(BF)

    adapter_part = jnp.dot(rotated, lowrank_down_map, preferred_element_type=F32)
    adapter_column = exchange(adapter_part.T.astype(BF), SLAB)
    adapter_column = adapter_column.astype(F32).sum(axis=0)

    by_depth = weights.reshape(stride, depth, cores, columns)
    own = lax.dynamic_index_in_dim(by_depth, core, 2, keepdims=False).reshape(stride, depth * columns)
    other = lax.dynamic_index_in_dim(by_depth, 1 - core, 2, keepdims=False).reshape(
        stride, depth * columns
    )
    part_other = jnp.dot(rotated, other, preferred_element_type=F32).astype(BF)
    part_own = jnp.dot(rotated, own, preferred_element_type=F32)
    arrived = lax.ppermute(part_other, "c", [(0, 1), (1, 0)])
    pair = (part_own + arrived.astype(F32)).astype(BF)
    pair = pair.reshape(slot_rows, depth, columns).transpose(1, 0, 2)
    frozen = exchange(pair, "z").astype(F32).sum(axis=0)

    d_full = gathered[:slot_rows]
    lowrank_full = gathered[slot_rows:]
    adapter_grad = LOWRANK_SCALE * lax.dot_general(
        d_full, lowrank_full, (((1,), (1,)), ((), ())), preferred_element_type=F32
    )
    d_rotated = lax.dot_general(
        d_full, weights, (((1,), (1,)), ((), ())), preferred_element_type=F32
    ) + lax.dot_general(
        adapter_grad.astype(BF),
        lowrank_down_map,
        (((1,), (1,)), ((), ())),
        preferred_element_type=F32,
    )
    row_product = jnp.sum(rotated.astype(F32) * d_rotated, axis=1)
    down_map_gradient = lax.dot_general(
        rotated, adapter_grad.astype(BF), (((0,), (0,)), ((), ())), preferred_element_type=F32
    )
    d_local = jnp.dot(d_rotated.astype(BF), spread_local, preferred_element_type=F32)
    chunk_rows = slot_rows * stride // (peers * LANES)
    riders = jnp.concatenate(
        [adapter_column, row_product, jnp.zeros((3 * LANES - 2 * slot_rows,), F32)]
    ).astype(BF)
    riders = jnp.broadcast_to(riders.reshape(1, 3, LANES), (peers, 3, LANES))
    d_chunks = jnp.concatenate([to_chunks((d_local * scaling).astype(BF), peers), riders], axis=1)
    d_chunks = exchange(d_chunks, SLAB)
    d_mixed = exchange(mix_blocks(d_chunks[:, :chunk_rows]), SLAB)
    hidden_gradient = (
        from_chunks(d_mixed, slot_rows, stride).astype(F32) * sign_values
    ).astype(BF)
    riders = d_chunks[:, chunk_rows:].reshape(peers, 3 * LANES)
    adapter_in = riders[:, :slot_rows]
    row_total = riders[:, slot_rows : 2 * slot_rows].astype(F32).sum(axis=0)

    slot_output = frozen + (LOWRANK_SCALE / replicas) * lax.dot_general(
        adapter_in, lowrank_local, (((0,), (0,)), ((), ())), preferred_element_type=F32
    )
    share = rank // replicas
    adapter_share = lax.dynamic_slice_in_dim(adapter_in, replica * share, share, 0)
    up_share = LOWRANK_SCALE * jnp.dot(adapter_share, d_rows, preferred_element_type=F32)
    total_high = row_total.astype(BF)
    total_low = (row_total - total_high.astype(F32)).astype(BF)
    totals = jnp.concatenate(
        [total_high.reshape(devices, capacity), total_low.reshape(devices, capacity)], axis=1
    )
    totals = jnp.pad(totals, ((0, 0), (0, columns - 2 * capacity)))[:, None, :]
    parcel = jnp.concatenate(
        [
            slot_output.astype(BF).reshape(devices, capacity, columns),
            totals,
            jnp.broadcast_to(up_share.astype(BF)[None], (devices, share, columns)),
        ],
        axis=1,
    )
    parcel = exchange(parcel, EXPERT)
    up_map_gradient = (
        parcel[:, capacity + 1 :].astype(F32).reshape(EXPERT_COUNT, rank, columns)
    )
    summed = (
        parcel[:, :capacity]
        .astype(F32)
        .reshape(EXPERT_COUNT, replicas, capacity, columns)
        .sum(axis=1)
        .reshape(EXPERT_COUNT * capacity, columns)
    )
    totals = parcel.reshape(EXPERT_COUNT, replicas, capacity + 1 + share, columns)[:, 0, capacity]
    totals = totals[:, : 2 * capacity].astype(F32)
    totals = (totals[:, :capacity] + totals[:, capacity:]).reshape(EXPERT_COUNT * capacity)
    slot_id = jnp.arange(EXPERT_COUNT * capacity, dtype=jnp.int32)
    chosen = target[:, None] == slot_id[None, :]
    gates_gradient = jnp.sum(jnp.where(chosen, totals[None, :], 0.0), axis=1)
    gates_gradient = gates_gradient.reshape(tokens_here, 2) / gates
    chosen = chosen.reshape(tokens_here, 2, EXPERT_COUNT * capacity)
    mixer = jnp.sum(jnp.where(chosen, gates[:, :, None], 0.0), axis=1)
    mixed = jnp.dot(mixer, summed, precision=HIGH_ACCURACY).astype(BF)
    return (mixed, hidden_gradient, down_map_gradient, up_map_gradient, gates_gradient)


def solution(mesh):
    owners, tensor = mesh.devices.shape
    split = Mesh(
        mesh.devices.reshape(EXPERT_COUNT, owners // EXPERT_COUNT, tensor // 2, 2),
        ("e", "r", "z", "c"),
    )
    every = EXPERT + TENSOR
    placed = (
        P(None, every),
        P(every, None),
        P(every, None),
        P(every),
        P(every, None),
        P(None, None, TENSOR),
        P(EXPERT, None),
        P(EXPERT, None),
        P(EXPERT, TENSOR),
    )
    return jax.shard_map(
        body,
        mesh=split,
        in_specs=placed,
        out_specs=(
            P(EXPERT, TENSOR),
            P(None, every),
            P(every, None),
            P(None, None, TENSOR),
            P(EXPERT, None),
        ),
        check_vma=False,
    )
```

```python
import math

import jax
import jax.numpy as jnp
import numpy as np
from jax import lax
from jax.sharding import Mesh
from jax.sharding import PartitionSpec as P

HIDDEN_UNITS = 16384
EXPERT_COUNT = 8
LOWRANK_SCALE = 0.5
HIGH_ACCURACY = lax.Precision.HIGHEST
BF = jnp.bfloat16
F32 = jnp.float32
EXPERT = ("e", "r")
TENSOR = ("z", "c")
LANES = 128


def sylvester(count):
    table = np.ones((1, 1), np.float32)
    while table.shape[0] < count:
        table = np.kron(np.array([[1.0, 1.0], [1.0, -1.0]], np.float32), table)
    return jnp.asarray(table, BF)


def exchange(value, axes):
    return lax.all_to_all(value, axes, split_axis=0, concat_axis=0, tiled=True)


def swapped(value, axis, bit):
    size = lax.axis_size(axis)
    return lax.ppermute(value, axis, [(i, i ^ 1 << bit) for i in range(size)])


def split(values):
    high = lax.reduce_precision(values, 8, 7)
    return high, lax.reduce_precision(values - high, 8, 7)


def butterfly(values, axis, bit, sums=(), exact=(), wire=BF):
    own = jnp.where(lax.axis_index(axis) // (1 << bit) % 2 == 1, -1.0, 1.0)
    parts = [values, *sums]
    for item in exact:
        parts += split(item) if wire == BF else [item]
    width = sum(part.shape[1] for part in parts)
    if width % LANES:
        parts.append(jnp.zeros((values.shape[0], -width % LANES), F32))
    message = jnp.concatenate(parts, axis=1) if len(parts) > 1 else values
    arrived = swapped(message.astype(wire), axis, bit).astype(F32)
    start = values.shape[1]
    values = arrived[:, :start] + own * values
    new_sums, new_exact = [], []
    for item in sums:
        new_sums.append(item + arrived[:, start : start + item.shape[1]])
        start += item.shape[1]
    for item in exact:
        size = item.shape[1]
        if wire == BF:
            high, low = split(item)
            other = arrived[:, start : start + size] + arrived[:, start + size : start + 2 * size]
            new_exact.append((high + low) + other)
            start += 2 * size
        else:
            new_exact.append(item + arrived[:, start : start + size])
            start += size
    return values, tuple(new_sums), tuple(new_exact)


def body(
    hidden, codes, scales, signs, lowrank_down_map, lowrank_up_map, experts, gates, output_gradient
):
    slot_rows, stride = hidden.shape
    replicas, depth, cores = lax.axis_size("r"), lax.axis_size("z"), lax.axis_size("c")
    devices = EXPERT_COUNT * replicas
    rank = lowrank_down_map.shape[1]
    expert_position = lax.axis_index("e")
    replica = lax.axis_index("r")
    core = lax.axis_index("c")
    capacity = slot_rows // devices
    tokens_here = experts.shape[0]
    columns = output_gradient.shape[1]
    scaling = 1.0 / math.sqrt(HIDDEN_UNITS)
    sign_values = (2 * signs - 1).astype(F32)
    group_size = codes.shape[0] // scales.shape[0]

    flat_ids = experts.reshape(tokens_here * 2)
    assigned = (flat_ids[:, None] == jnp.arange(EXPERT_COUNT, dtype=jnp.int32)[None, :]).astype(
        jnp.int32
    )
    earlier = jnp.cumsum(assigned, axis=0) - assigned
    slot_index = jnp.sum(earlier * assigned, axis=1)
    target = flat_ids * capacity + slot_index
    row = jnp.arange(devices * capacity, dtype=jnp.int32)
    row_slot = row // (replicas * capacity) * capacity + row % capacity
    copier = (row_slot[:, None] == target[None, :]).astype(BF)
    weighted = (
        (gates[:, :, None] * output_gradient.astype(F32)[:, None, :])
        .reshape(tokens_here * 2, columns)
        .astype(BF)
    )
    outgoing = jnp.dot(copier, weighted, preferred_element_type=F32).astype(BF)
    d_rows = exchange(outgoing, EXPERT)
    lowrank_local = lax.dynamic_index_in_dim(lowrank_up_map, expert_position, 0, keepdims=False)
    d_own = exchange(jnp.broadcast_to(d_rows[None], (depth, slot_rows, columns)), "z")
    d_other = swapped(d_own, "c", 0)

    spread_local = sylvester(stride)
    signed = (hidden.astype(F32) * sign_values).astype(BF)
    state = jnp.dot(signed, spread_local, preferred_element_type=F32)
    for bit in range(replicas.bit_length() - 1):
        state, _, _ = butterfly(state, "r", bit, wire=F32)
    adapter_grad = LOWRANK_SCALE * lax.dot_general(
        d_rows, lowrank_local, (((1,), (1,)), ((), ())), preferred_element_type=F32
    )
    state, _, (adapter_grad,) = butterfly(state, "c", 0, exact=(adapter_grad,), wire=F32)
    for bit in range(depth.bit_length() - 1):
        state, _, (adapter_grad,) = butterfly(state, "z", bit, exact=(adapter_grad,))
    rotated = (state * scaling).astype(BF)

    weights = (codes.astype(F32) * jnp.repeat(scales, group_size, axis=0)).astype(BF)
    adapter_part = jnp.dot(rotated, lowrank_down_map, preferred_element_type=F32)

    by_depth = weights.reshape(stride, depth, cores, columns)
    own = lax.dynamic_index_in_dim(by_depth, core, 2, keepdims=False)
    other = lax.dynamic_index_in_dim(by_depth, 1 - core, 2, keepdims=False)

    def forward(part):
        return jnp.einsum("sk,kzf->zsf", rotated, part, preferred_element_type=F32)

    arrived = swapped(forward(other).astype(BF), "c", 0)
    pair = (forward(own) + arrived.astype(F32)).astype(BF)

    def backward(cotangent, part):
        return jnp.einsum("zsf,kzf->sk", cotangent, part, preferred_element_type=F32)

    d_rotated = (
        backward(d_own, own)
        + backward(d_other, other)
        + lax.dot_general(
            adapter_grad.astype(BF),
            lowrank_down_map,
            (((1,), (1,)), ((), ())),
            preferred_element_type=F32,
        )
    )
    row_product = jnp.sum(rotated.astype(F32) * d_rotated, axis=1, keepdims=True)
    down_map_gradient = lax.dot_general(
        rotated, adapter_grad.astype(BF), (((0,), (0,)), ((), ())), preferred_element_type=F32
    )
    d_local = jnp.dot(d_rotated.astype(BF), spread_local, preferred_element_type=F32)
    d_local, pair = lax.optimization_barrier((d_local, pair))
    frozen = exchange(pair, "z").astype(F32).sum(axis=0)
    state, sums, exact = d_local, (adapter_part,), (row_product,)
    for bit in range(replicas.bit_length() - 1):
        state, sums, exact = butterfly(state, "r", bit, sums, exact)
    state, sums, exact = butterfly(state, "c", 0, sums, exact, wire=F32)
    for bit in range(depth.bit_length() - 1):
        state, sums, exact = butterfly(state, "z", bit, sums, exact)
    hidden_gradient = (state * (sign_values * scaling)[None, :]).astype(BF)
    adapter_in = sums[0]
    row_total = exact[0][:, 0]

    slot_output = frozen + (LOWRANK_SCALE / replicas) * jnp.dot(
        adapter_in.astype(BF), lowrank_local, preferred_element_type=F32
    )
    share = rank // replicas
    adapter_share = lax.dynamic_slice_in_dim(adapter_in, replica * share, share, 1)
    adapter_share = jnp.concatenate(split(adapter_share), axis=1).astype(BF)
    up_share = LOWRANK_SCALE * lax.dot_general(
        adapter_share, d_rows, (((0,), (0,)), ((), ())), preferred_element_type=F32
    )
    up_share = up_share[:share] + up_share[share:]
    totals = jnp.concatenate(
        [part.astype(BF).reshape(devices, capacity) for part in split(row_total)], axis=1
    )
    totals = jnp.pad(totals, ((0, 0), (0, columns - 2 * capacity)))[:, None, :]
    parcel = jnp.concatenate(
        [
            slot_output.astype(BF).reshape(devices, capacity, columns),
            totals,
            jnp.broadcast_to(up_share.astype(BF)[None], (devices, share, columns)),
        ],
        axis=1,
    )
    parcel = exchange(parcel, EXPERT)
    up_map_gradient = (
        parcel[:, capacity + 1 :].astype(F32).reshape(EXPERT_COUNT, rank, columns)
    )
    summed = (
        parcel[:, :capacity]
        .astype(F32)
        .reshape(EXPERT_COUNT, replicas, capacity, columns)
        .sum(axis=1)
        .reshape(EXPERT_COUNT * capacity, columns)
    )
    totals = parcel.reshape(EXPERT_COUNT, replicas, capacity + 1 + share, columns)[:, 0, capacity]
    totals = totals[:, : 2 * capacity].astype(F32)
    totals = (totals[:, :capacity] + totals[:, capacity:]).reshape(EXPERT_COUNT * capacity)
    slot_id = jnp.arange(EXPERT_COUNT * capacity, dtype=jnp.int32)
    chosen = target[:, None] == slot_id[None, :]
    gates_gradient = jnp.sum(jnp.where(chosen, totals[None, :], 0.0), axis=1)
    gates_gradient = gates_gradient.reshape(tokens_here, 2) / gates
    chosen = chosen.reshape(tokens_here, 2, EXPERT_COUNT * capacity)
    mixer = jnp.sum(jnp.where(chosen, gates[:, :, None], 0.0), axis=1)
    mixed = jnp.dot(mixer, summed, precision=HIGH_ACCURACY).astype(BF)
    return (mixed, hidden_gradient, down_map_gradient, up_map_gradient, gates_gradient)


def solution(mesh):
    owners, tensor = mesh.devices.shape
    split = Mesh(
        mesh.devices.reshape(EXPERT_COUNT, owners // EXPERT_COUNT, tensor // 2, 2),
        ("e", "r", "z", "c"),
    )
    every = EXPERT + TENSOR
    placed = (
        P(None, every),
        P(every, None),
        P(every, None),
        P(every),
        P(every, None),
        P(None, None, TENSOR),
        P(EXPERT, None),
        P(EXPERT, None),
        P(EXPERT, TENSOR),
    )
    return jax.shard_map(
        body,
        mesh=split,
        in_specs=placed,
        out_specs=(
            P(EXPERT, TENSOR),
            P(None, every),
            P(every, None),
            P(None, None, TENSOR),
            P(EXPERT, None),
        ),
        check_vma=False,
    )
```

```python
import math

import jax
import jax.numpy as jnp
import numpy as np
from jax import lax
from jax.sharding import Mesh
from jax.sharding import PartitionSpec as P

HIDDEN_UNITS = 16384
EXPERT_COUNT = 8
LOWRANK_SCALE = 0.5
HIGH_ACCURACY = lax.Precision.HIGHEST
BF = jnp.bfloat16
F32 = jnp.float32
EXPERT = ("e", "r")
TENSOR = ("z", "c")
SLAB = ("r", "z", "c")
LANES = 128


def sylvester(count):
    table = np.ones((1, 1), np.float32)
    while table.shape[0] < count:
        table = np.kron(np.array([[1.0, 1.0], [1.0, -1.0]], np.float32), table)
    return jnp.asarray(table, BF)


def exchange(value, axes):
    return lax.all_to_all(value, axes, split_axis=0, concat_axis=0, tiled=True)


def to_chunks(values, peers):
    height, stride = values.shape
    halves = stride // LANES
    blocks = peers // halves
    shaped = values.reshape(blocks, height // blocks, halves, LANES)
    return shaped.transpose(0, 2, 1, 3).reshape(peers, height // blocks, LANES)


def from_chunks(chunks, height, stride):
    halves = stride // LANES
    blocks = chunks.shape[0] // halves
    shaped = chunks.reshape(blocks, halves, height // blocks, LANES)
    return shaped.transpose(0, 2, 1, 3).reshape(height, stride)


def split(values):
    high = lax.reduce_precision(values, 8, 7)
    return high, lax.reduce_precision(values - high, 8, 7)


def mix_blocks(chunks):
    peers, rows, lanes = chunks.shape
    mixed = jnp.dot(
        sylvester(peers), chunks.reshape(peers, rows * lanes), preferred_element_type=F32
    )
    return mixed.astype(BF).reshape(peers, rows, lanes)


def body(
    hidden, codes, scales, signs, lowrank_down_map, lowrank_up_map, experts, gates, output_gradient
):
    slot_rows, stride = hidden.shape
    replicas, depth, cores = lax.axis_size("r"), lax.axis_size("z"), lax.axis_size("c")
    devices = EXPERT_COUNT * replicas
    peers = replicas * depth * cores
    rank = lowrank_down_map.shape[1]
    expert_position = lax.axis_index("e")
    replica = lax.axis_index("r")
    core = lax.axis_index("c")
    capacity = slot_rows // devices
    tokens_here = experts.shape[0]
    columns = output_gradient.shape[1]
    scaling = 1.0 / math.sqrt(HIDDEN_UNITS)
    sign_values = (2 * signs - 1).astype(F32)
    group_size = codes.shape[0] // scales.shape[0]

    flat_ids = experts.reshape(tokens_here * 2)
    assigned = (flat_ids[:, None] == jnp.arange(EXPERT_COUNT, dtype=jnp.int32)[None, :]).astype(
        jnp.int32
    )
    earlier = jnp.cumsum(assigned, axis=0) - assigned
    slot_index = jnp.sum(earlier * assigned, axis=1)
    target = flat_ids * capacity + slot_index
    row = jnp.arange(devices * capacity, dtype=jnp.int32)
    row_slot = row // (replicas * capacity) * capacity + row % capacity
    copier = (row_slot[:, None] == target[None, :]).astype(BF)
    weighted = (
        (gates[:, :, None] * output_gradient.astype(F32)[:, None, :])
        .reshape(tokens_here * 2, columns)
        .astype(BF)
    )
    outgoing = jnp.dot(copier, weighted, preferred_element_type=F32).astype(BF)
    d_rows = exchange(outgoing, EXPERT)
    lowrank_local = lax.dynamic_index_in_dim(lowrank_up_map, expert_position, 0, keepdims=False)
    gathered = lax.all_gather(
        jnp.concatenate([d_rows, lowrank_local], axis=0), TENSOR, axis=1, tiled=True
    )

    signed = (hidden.astype(F32) * sign_values).astype(BF)
    mixed_blocks = mix_blocks(exchange(to_chunks(signed, peers), SLAB))
    unrotated = from_chunks(exchange(mixed_blocks, SLAB), slot_rows, stride)
    spread_local = sylvester(stride)
    rotated = (jnp.dot(unrotated, spread_local, preferred_element_type=F32) * scaling).astype(BF)

    weights = (codes.astype(F32) * jnp.repeat(scales, group_size, axis=0)).astype(BF)

    adapter_part = jnp.dot(rotated, lowrank_down_map, preferred_element_type=F32)

    by_depth = weights.reshape(stride, depth, cores, columns)
    own = lax.dynamic_index_in_dim(by_depth, core, 2, keepdims=False).reshape(stride, depth * columns)
    other = lax.dynamic_index_in_dim(by_depth, 1 - core, 2, keepdims=False).reshape(
        stride, depth * columns
    )
    part_other = jnp.dot(rotated, other, preferred_element_type=F32).astype(BF)
    part_own = jnp.dot(rotated, own, preferred_element_type=F32)
    arrived = lax.ppermute(part_other, "c", [(0, 1), (1, 0)])
    pair = part_own + arrived.astype(F32)
    pair = pair.reshape(slot_rows, depth, columns).transpose(1, 0, 2)
    frozen = lax.psum_scatter(pair, "z", scatter_dimension=0, tiled=False)

    d_full = gathered[:slot_rows]
    lowrank_full = gathered[slot_rows:]
    adapter_grad = LOWRANK_SCALE * lax.dot_general(
        d_full, lowrank_full, (((1,), (1,)), ((), ())), preferred_element_type=F32
    )
    d_rotated = lax.dot_general(
        d_full, weights, (((1,), (1,)), ((), ())), preferred_element_type=F32
    ) + lax.dot_general(
        adapter_grad.astype(BF),
        lowrank_down_map,
        (((1,), (1,)), ((), ())),
        preferred_element_type=F32,
    )
    row_product = jnp.sum(rotated.astype(F32) * d_rotated, axis=1)
    down_map_gradient = lax.dot_general(
        rotated, adapter_grad.astype(BF), (((0,), (0,)), ((), ())), preferred_element_type=F32
    )
    d_local = jnp.dot(d_rotated.astype(BF), spread_local, preferred_element_type=F32)
    chunk_rows = slot_rows * stride // (peers * LANES)
    riders = jnp.concatenate(
        [
            adapter_part.T,
            jnp.broadcast_to(row_product[None], (peers, slot_rows)),
            jnp.zeros((peers, 3 * LANES - 2 * slot_rows), F32),
        ],
        axis=1,
    ).astype(BF)
    d_chunks = to_chunks((d_local * scaling).astype(BF), peers)
    d_chunks = jnp.concatenate([d_chunks, riders.reshape(peers, 3, LANES)], axis=1)
    d_chunks = exchange(d_chunks, SLAB)
    riders = d_chunks[:, chunk_rows:].astype(F32).sum(axis=0).reshape(3 * LANES)
    row_total = riders[slot_rows : 2 * slot_rows]
    column = jnp.pad(riders[:slot_rows], (0, 2 * LANES - slot_rows)).astype(BF)
    column = jnp.broadcast_to(column.reshape(1, 2, LANES), (peers, 2, LANES))
    d_mixed = jnp.concatenate([mix_blocks(d_chunks[:, :chunk_rows]), column], axis=1)
    d_mixed = exchange(d_mixed, SLAB)
    hidden_gradient = (
        from_chunks(d_mixed[:, :chunk_rows], slot_rows, stride).astype(F32) * sign_values
    ).astype(BF)
    adapter_in = d_mixed[:, chunk_rows:].reshape(peers, 2 * LANES)[:, :slot_rows]

    slot_output = frozen + (LOWRANK_SCALE / replicas) * lax.dot_general(
        adapter_in, lowrank_local, (((0,), (0,)), ((), ())), preferred_element_type=F32
    )
    share = rank // replicas
    adapter_share = lax.dynamic_slice_in_dim(adapter_in, replica * share, share, 0)
    up_share = LOWRANK_SCALE * jnp.dot(adapter_share, d_rows, preferred_element_type=F32)
    totals = jnp.concatenate(
        [part.astype(BF).reshape(devices, capacity) for part in split(row_total)], axis=1
    )
    totals = jnp.pad(totals, ((0, 0), (0, columns - 2 * capacity)))[:, None, :]
    parcel = jnp.concatenate(
        [
            slot_output.astype(BF).reshape(devices, capacity, columns),
            totals,
            jnp.broadcast_to(up_share.astype(BF)[None], (devices, share, columns)),
        ],
        axis=1,
    )
    parcel = exchange(parcel, EXPERT)
    up_map_gradient = (
        parcel[:, capacity + 1 :].astype(F32).reshape(EXPERT_COUNT, rank, columns)
    )
    summed = (
        parcel[:, :capacity]
        .astype(F32)
        .reshape(EXPERT_COUNT, replicas, capacity, columns)
        .sum(axis=1)
        .reshape(EXPERT_COUNT * capacity, columns)
    )
    totals = parcel.reshape(EXPERT_COUNT, replicas, capacity + 1 + share, columns)[:, 0, capacity]
    totals = totals[:, : 2 * capacity].astype(F32)
    totals = (totals[:, :capacity] + totals[:, capacity:]).reshape(EXPERT_COUNT * capacity)
    slot_id = jnp.arange(EXPERT_COUNT * capacity, dtype=jnp.int32)
    chosen = target[:, None] == slot_id[None, :]
    gates_gradient = jnp.sum(jnp.where(chosen, totals[None, :], 0.0), axis=1)
    gates_gradient = gates_gradient.reshape(tokens_here, 2) / gates
    chosen = chosen.reshape(tokens_here, 2, EXPERT_COUNT * capacity)
    mixer = jnp.sum(jnp.where(chosen, gates[:, :, None], 0.0), axis=1)
    mixed = jnp.dot(mixer, summed, precision=HIGH_ACCURACY).astype(BF)
    return (mixed, hidden_gradient, down_map_gradient, up_map_gradient, gates_gradient)


def solution(mesh):
    owners, tensor = mesh.devices.shape
    split = Mesh(
        mesh.devices.reshape(EXPERT_COUNT, owners // EXPERT_COUNT, tensor // 2, 2),
        ("e", "r", "z", "c"),
    )
    every = EXPERT + TENSOR
    placed = (
        P(None, every),
        P(every, None),
        P(every, None),
        P(every),
        P(every, None),
        P(None, None, TENSOR),
        P(EXPERT, None),
        P(EXPERT, None),
        P(EXPERT, TENSOR),
    )
    return jax.shard_map(
        body,
        mesh=split,
        in_specs=placed,
        out_specs=(
            P(EXPERT, TENSOR),
            P(None, every),
            P(every, None),
            P(None, None, TENSOR),
            P(EXPERT, None),
        ),
        check_vma=False,
    )
```

```python
import math

import jax
import jax.numpy as jnp
import numpy as np
from jax import lax
from jax.experimental import pallas as pl
from jax.experimental.pallas import tpu as pltpu
from jax.sharding import Mesh
from jax.sharding import PartitionSpec as P

HIDDEN_UNITS = 16384
EXPERT_COUNT = 8
LOWRANK_SCALE = 0.5
HIGH_ACCURACY = lax.Precision.HIGHEST
BF = jnp.bfloat16
F32 = jnp.float32
EXPERT = ("e", "r")
TENSOR = ("z", "c")
SLAB = ("r", "z", "c")
LANES = 128
TILE = 8
ROWS = 5


def sylvester(count):
    table = np.ones((1, 1), np.float32)
    while table.shape[0] < count:
        table = np.kron(np.array([[1.0, 1.0], [1.0, -1.0]], np.float32), table)
    return jnp.asarray(table, BF)


def exchange(value, axes):
    return lax.all_to_all(value, axes, split_axis=0, concat_axis=0, tiled=True)


def dot(left, right, dims=((1,), (0,))):
    return lax.dot_general(left, right, (dims, ((), ())), preferred_element_type=F32)


def placement(blocks, rows):
    out_row = lax.broadcasted_iota(jnp.int32, (blocks * TILE, blocks * rows), 0)
    in_row = lax.broadcasted_iota(jnp.int32, (blocks * TILE, blocks * rows), 1)
    k = out_row % TILE
    return jnp.where((k < rows) & (out_row // TILE * rows + k == in_row), 1.0, 0.0).astype(BF)


def rider_rows(peers, k):
    out_row = lax.broadcasted_iota(jnp.int32, (peers * TILE, peers), 0)
    in_row = lax.broadcasted_iota(jnp.int32, (peers * TILE, peers), 1)
    return jnp.where(out_row == in_row * TILE + k, 1.0, 0.0).astype(BF)


def whole(kernel, out_shape, *operands):
    return pl.pallas_call(
        kernel,
        out_shape=out_shape,
        compiler_params=pltpu.CompilerParams(vmem_limit_bytes=32 * 1024 * 1024),
    )(*operands)


def to_chunks(values, signs):
    height, stride = values.shape
    halves = stride // LANES
    blocks = height // ROWS

    def kernel(values_ref, signs_ref, out_ref):
        sign = (2 * signs_ref[...] - 1).astype(F32)
        signed = (values_ref[...].astype(F32) * sign).astype(BF)
        place = placement(blocks, ROWS)
        for half in range(halves):
            part = dot(place, signed[:, half * LANES : (half + 1) * LANES])
            part = part.astype(BF).reshape(blocks, TILE, LANES)
            out_ref[half * blocks : (half + 1) * blocks] = part

    out = jax.ShapeDtypeStruct((halves * blocks, TILE, LANES), BF)
    return whole(kernel, out, values, signs.reshape(1, stride))


def hadamard(parts):
    step = 1
    while step < len(parts):
        for low in range(len(parts)):
            if low & step == 0:
                one, two = parts[low], parts[low + step]
                parts[low], parts[low + step] = one + two, one - two
        step *= 2
    return parts


def mix_blocks(chunks):
    def kernel(chunks_ref, out_ref, sum_ref):
        values = chunks_ref[...].astype(F32)
        mixed = hadamard([values[p] for p in range(values.shape[0])])
        row = lax.broadcasted_iota(jnp.int32, (TILE, LANES), 0)
        sum_ref[...] = mixed[0]
        for p, part in enumerate(mixed):
            out_ref[p] = jnp.where(row < ROWS, part, mixed[0]).astype(BF)

    out = jax.ShapeDtypeStruct(chunks.shape, BF), jax.ShapeDtypeStruct((TILE, LANES), F32)
    return whole(kernel, out, chunks)


def gather_rows(chunks, blocks):
    flat = chunks.reshape(-1, LANES)
    place = placement(blocks, ROWS)
    size = blocks * TILE
    halves = flat.shape[0] // size
    parts = [
        dot(place, flat[half * size : (half + 1) * size], ((0,), (0,))) for half in range(halves)
    ]
    return jnp.concatenate(parts, axis=1)


def finish_rotation(chunks, spread, scaling):
    blocks = chunks.shape[0] * LANES // spread.shape[0]

    def kernel(chunks_ref, spread_ref, out_ref):
        values = gather_rows(chunks_ref[...], blocks).astype(BF)
        out_ref[...] = (dot(values, spread_ref[...]) * scaling).astype(BF)

    out = jax.ShapeDtypeStruct((blocks * ROWS, spread.shape[0]), BF)
    return whole(kernel, out, chunks, spread)


def finish_gradient(chunks, signs):
    stride = signs.shape[0]
    blocks = chunks.shape[0] * LANES // stride

    def kernel(chunks_ref, signs_ref, out_ref):
        sign = (2 * signs_ref[...] - 1).astype(F32)
        out_ref[...] = (gather_rows(chunks_ref[...], blocks) * sign).astype(BF)

    out = jax.ShapeDtypeStruct((blocks * ROWS, stride), BF)
    return whole(kernel, out, chunks, signs.reshape(1, stride))


def backward_chunks(main, adapter_grad, down_map, rotated, spread, scaling):
    height, stride = main.shape
    halves = stride // LANES
    blocks = height // ROWS
    peers = halves * blocks
    rest = height - LANES

    def kernel(main_ref, grad_ref, down_ref, rotated_ref, spread_ref, out_ref):
        rotated_value = rotated_ref[...]
        down = down_ref[...]
        d_rotated = main_ref[...] + dot(grad_ref[...], down, ((1,), (1,)))
        local = dot(d_rotated.astype(BF), spread_ref[...])
        local = (local * scaling).astype(BF)
        product = rotated_value.astype(F32) * d_rotated
        totals = lax.dot_general(
            jnp.ones((TILE, stride), F32),
            product,
            (((1,), (1,)), ((), ())),
            precision=HIGH_ACCURACY,
            preferred_element_type=F32,
        )
        adapter = dot(down, rotated_value, ((0,), (1,))).astype(BF)
        pad = jnp.zeros((peers, LANES - rest), BF)
        riders = dot(rider_rows(peers, ROWS), adapter[:, :LANES])
        tail = jnp.concatenate([adapter[:, LANES:], pad], axis=1)
        riders += dot(rider_rows(peers, ROWS + 1), tail)
        row_tail = jnp.concatenate(
            [totals[:, LANES:], jnp.zeros((TILE, LANES - rest), F32)], axis=1
        )
        row_tail = pltpu.roll(row_tail, rest, 1)
        k = lax.broadcasted_iota(jnp.int32, (TILE, LANES), 0)
        extra = jnp.where(k == ROWS + 2, totals[:, :LANES], 0.0)
        extra += jnp.where(k == ROWS + 1, row_tail, 0.0)
        place = placement(blocks, ROWS)
        for half in range(halves):
            part = dot(place, local[:, half * LANES : (half + 1) * LANES])
            part += riders[half * blocks * TILE : (half + 1) * blocks * TILE]
            part = part.reshape(blocks, TILE, LANES) + extra[None]
            out_ref[half * blocks : (half + 1) * blocks] = part.astype(BF)

    out = jax.ShapeDtypeStruct((peers, TILE, LANES), BF)
    return whole(kernel, out, main, adapter_grad, down_map, rotated, spread)


def split(values):
    high = lax.reduce_precision(values, 8, 7)
    return high, lax.reduce_precision(values - high, 8, 7)


def body(
    hidden, codes, scales, signs, lowrank_down_map, lowrank_up_map, experts, gates, output_gradient
):
    slot_rows, stride = hidden.shape
    replicas, depth, cores = lax.axis_size("r"), lax.axis_size("z"), lax.axis_size("c")
    devices = EXPERT_COUNT * replicas
    rank = lowrank_down_map.shape[1]
    expert_position = lax.axis_index("e")
    replica = lax.axis_index("r")
    core = lax.axis_index("c")
    capacity = slot_rows // devices
    tokens_here = experts.shape[0]
    columns = output_gradient.shape[1]
    scaling = 1.0 / math.sqrt(HIDDEN_UNITS)
    group_size = codes.shape[0] // scales.shape[0]

    flat_ids = experts.reshape(tokens_here * 2)
    assigned = (flat_ids[:, None] == jnp.arange(EXPERT_COUNT, dtype=jnp.int32)[None, :]).astype(
        jnp.int32
    )
    earlier = jnp.cumsum(assigned, axis=0) - assigned
    slot_index = jnp.sum(earlier * assigned, axis=1)
    target = flat_ids * capacity + slot_index
    row = jnp.arange(devices * capacity, dtype=jnp.int32)
    row_slot = row // (replicas * capacity) * capacity + row % capacity
    copier = (row_slot[:, None] == target[None, :]).astype(BF)
    weighted = (
        (gates[:, :, None] * output_gradient.astype(F32)[:, None, :])
        .reshape(tokens_here * 2, columns)
        .astype(BF)
    )
    outgoing = jnp.dot(copier, weighted, preferred_element_type=F32).astype(BF)
    d_rows = exchange(outgoing, EXPERT)
    lowrank_local = lax.dynamic_index_in_dim(lowrank_up_map, expert_position, 0, keepdims=False)
    gathered = lax.all_gather(
        jnp.concatenate([d_rows, lowrank_local], axis=0), TENSOR, axis=1, tiled=True
    )

    spread_local = sylvester(stride)
    mixed_blocks, _ = mix_blocks(exchange(to_chunks(hidden, signs), SLAB))
    rotated = finish_rotation(exchange(mixed_blocks, SLAB), spread_local, scaling)

    weights = (codes.astype(F32) * jnp.repeat(scales, group_size, axis=0)).astype(BF)
    by_depth = weights.reshape(stride, depth, cores, columns)
    own = lax.dynamic_index_in_dim(by_depth, core, 2, keepdims=False)
    other = lax.dynamic_index_in_dim(by_depth, 1 - core, 2, keepdims=False)
    other = lax.ppermute(other, "c", [(0, 1), (1, 0)])
    neighbour = lax.ppermute(rotated, "c", [(0, 1), (1, 0)])
    pair = jnp.einsum("sk,kzf->zsf", rotated, own, preferred_element_type=F32)
    pair = pair + jnp.einsum("sk,kzf->zsf", neighbour, other, preferred_element_type=F32)
    frozen = lax.psum_scatter(pair, "z", scatter_dimension=0, tiled=False)

    d_full = gathered[:slot_rows]
    lowrank_full = gathered[slot_rows:]
    adapter_grad = LOWRANK_SCALE * lax.dot_general(
        d_full, lowrank_full, (((1,), (1,)), ((), ())), preferred_element_type=F32
    )
    adapter_grad = adapter_grad.astype(BF)
    main = dot(d_full, weights, ((1,), (1,)))
    down_map_gradient = dot(rotated, adapter_grad, ((0,), (0,)))
    d_chunks = exchange(
        backward_chunks(main, adapter_grad, lowrank_down_map, rotated, spread_local, scaling), SLAB
    )
    d_mixed, sums = mix_blocks(d_chunks)
    rest = slot_rows - LANES
    row_total = jnp.concatenate([sums[ROWS + 2], sums[ROWS + 1, rest : 2 * rest]])
    d_mixed = exchange(d_mixed, SLAB)
    hidden_gradient = finish_gradient(d_mixed, signs)
    adapter_in = jnp.concatenate([d_mixed[:, ROWS], d_mixed[:, ROWS + 1, :rest]], axis=1)

    slot_output = frozen + (LOWRANK_SCALE / replicas) * lax.dot_general(
        adapter_in, lowrank_local, (((0,), (0,)), ((), ())), preferred_element_type=F32
    )
    share = rank // replicas
    adapter_share = lax.dynamic_slice_in_dim(adapter_in, replica * share, share, 0)
    up_share = LOWRANK_SCALE * jnp.dot(adapter_share, d_rows, preferred_element_type=F32)
    totals = jnp.concatenate(
        [part.astype(BF).reshape(devices, capacity) for part in split(row_total)], axis=1
    )
    totals = jnp.pad(totals, ((0, 0), (0, columns - 2 * capacity)))[:, None, :]
    parcel = jnp.concatenate(
        [
            slot_output.astype(BF).reshape(devices, capacity, columns),
            totals,
            jnp.broadcast_to(up_share.astype(BF)[None], (devices, share, columns)),
        ],
        axis=1,
    )
    parcel = exchange(parcel, EXPERT)
    up_map_gradient = (
        parcel[:, capacity + 1 :].astype(F32).reshape(EXPERT_COUNT, rank, columns)
    )
    summed = (
        parcel[:, :capacity]
        .astype(F32)
        .reshape(EXPERT_COUNT, replicas, capacity, columns)
        .sum(axis=1)
        .reshape(EXPERT_COUNT * capacity, columns)
    )
    totals = parcel.reshape(EXPERT_COUNT, replicas, capacity + 1 + share, columns)[:, 0, capacity]
    totals = totals[:, : 2 * capacity].astype(F32)
    totals = (totals[:, :capacity] + totals[:, capacity:]).reshape(EXPERT_COUNT * capacity)
    slot_id = jnp.arange(EXPERT_COUNT * capacity, dtype=jnp.int32)
    chosen = target[:, None] == slot_id[None, :]
    gates_gradient = jnp.sum(jnp.where(chosen, totals[None, :], 0.0), axis=1)
    gates_gradient = gates_gradient.reshape(tokens_here, 2) / gates
    chosen = chosen.reshape(tokens_here, 2, EXPERT_COUNT * capacity)
    mixer = jnp.sum(jnp.where(chosen, gates[:, :, None], 0.0), axis=1)
    mixed = jnp.dot(mixer, summed, precision=HIGH_ACCURACY).astype(BF)
    return (mixed, hidden_gradient, down_map_gradient, up_map_gradient, gates_gradient)


def solution(mesh):
    owners, tensor = mesh.devices.shape
    split = Mesh(
        mesh.devices.reshape(EXPERT_COUNT, owners // EXPERT_COUNT, tensor // 2, 2),
        ("e", "r", "z", "c"),
    )
    every = EXPERT + TENSOR
    placed = (
        P(None, every),
        P(every, None),
        P(every, None),
        P(every),
        P(every, None),
        P(None, None, TENSOR),
        P(EXPERT, None),
        P(EXPERT, None),
        P(EXPERT, TENSOR),
    )
    return jax.shard_map(
        body,
        mesh=split,
        in_specs=placed,
        out_specs=(
            P(EXPERT, TENSOR),
            P(None, every),
            P(every, None),
            P(None, None, TENSOR),
            P(EXPERT, None),
        ),
        check_vma=False,
    )
```

```python
import math

import jax
import jax.numpy as jnp
import numpy as np
from jax import lax
from jax.experimental import pallas as pl
from jax.experimental.pallas import tpu as pltpu
from jax.sharding import Mesh
from jax.sharding import PartitionSpec as P

HIDDEN_UNITS = 16384
EXPERT_COUNT = 8
LOWRANK_SCALE = 0.5
HIGH_ACCURACY = lax.Precision.HIGHEST
BF = jnp.bfloat16
F32 = jnp.float32
EXPERT = ("e", "r")
TENSOR = ("z", "c")
SLAB = ("r", "z", "c")
LANES = 128
TILE = 8
ROWS = 5


def sylvester(count):
    table = np.ones((1, 1), np.float32)
    while table.shape[0] < count:
        table = np.kron(np.array([[1.0, 1.0], [1.0, -1.0]], np.float32), table)
    return jnp.asarray(table, BF)


def exchange(value, axes):
    return lax.all_to_all(value, axes, split_axis=0, concat_axis=0, tiled=True)


def dot(left, right, dims=((1,), (0,))):
    return lax.dot_general(left, right, (dims, ((), ())), preferred_element_type=F32)


def placement(blocks, rows):
    out_row = lax.broadcasted_iota(jnp.int32, (blocks * TILE, blocks * rows), 0)
    in_row = lax.broadcasted_iota(jnp.int32, (blocks * TILE, blocks * rows), 1)
    k = out_row % TILE
    return jnp.where((k < rows) & (out_row // TILE * rows + k == in_row), 1.0, 0.0).astype(BF)


def rider_rows(peers, k):
    out_row = lax.broadcasted_iota(jnp.int32, (peers * TILE, peers), 0)
    in_row = lax.broadcasted_iota(jnp.int32, (peers * TILE, peers), 1)
    return jnp.where(out_row == in_row * TILE + k, 1.0, 0.0).astype(BF)


def whole(kernel, out_shape, *operands):
    return pl.pallas_call(
        kernel,
        out_shape=out_shape,
        compiler_params=pltpu.CompilerParams(vmem_limit_bytes=32 * 1024 * 1024),
    )(*operands)


def route(experts, gates, output_gradient, row_slot, capacity):
    tokens, columns = output_gradient.shape
    choices = experts.shape[1]

    def kernel(experts_ref, gates_ref, grad_ref, row_slot_ref, out_ref, target_ref):
        ids = experts_ref[...]
        gate = gates_ref[...]
        grad = grad_ref[...].astype(F32)
        expert = lax.broadcasted_iota(jnp.int32, (tokens, EXPERT_COUNT), 1)
        named = [
            jnp.where(ids[:, k : k + 1] == expert, 1.0, 0.0) for k in range(choices)
        ]
        row = lax.broadcasted_iota(jnp.int32, (tokens, tokens), 0)
        col = lax.broadcasted_iota(jnp.int32, (tokens, tokens), 1)
        lower = jnp.where(row > col, 1.0, 0.0).astype(BF)
        earlier = dot(lower, sum(named).astype(BF))
        rows = 0.0
        targets = []
        for k in range(choices):
            slot = jnp.sum(earlier * named[k], axis=1, keepdims=True).astype(jnp.int32)
            target = ids[:, k : k + 1] * capacity + slot
            match = jnp.where(target == row_slot_ref[...], 1.0, 0.0).astype(BF)
            weighted = (gate[:, k : k + 1] * grad).astype(BF)
            rows = rows + dot(match, weighted, ((0,), (0,)))
            earlier = earlier + named[k]
            targets.append(target)
        out_ref[...] = rows.astype(BF)
        choice = lax.broadcasted_iota(jnp.int32, (tokens, choices), 1)
        chosen = targets[0]
        for k in range(1, choices):
            chosen = jnp.where(choice == k, targets[k], chosen)
        target_ref[...] = chosen

    out = (
        jax.ShapeDtypeStruct((row_slot.shape[1], columns), BF),
        jax.ShapeDtypeStruct((tokens, choices), jnp.int32),
    )
    return whole(kernel, out, experts, gates, output_gradient, row_slot)


def dequantize(codes, scales, depth, columns):
    stride, width = codes.shape
    groups = scales.shape[0]
    size = stride // groups

    def kernel(codes_ref, scales_ref, all_ref, own_ref, other_ref):
        first = lax.axis_index("c") == 0
        for group in range(groups):
            rows = slice(group * size, (group + 1) * size)
            values = codes_ref[rows, :].astype(F32) * scales_ref[group : group + 1, :]
            all_ref[rows, :] = values.astype(BF)
            low, high = values[:, :columns], values[:, columns:]
            own_ref[0, rows, :] = jnp.where(first, low, high).astype(BF)
            other_ref[0, rows, :] = jnp.where(first, high, low).astype(BF)

    half = pl.BlockSpec((1, stride, columns), lambda z: (z, 0, 0))
    halves = jax.ShapeDtypeStruct((depth, stride, columns), BF)
    return pl.pallas_call(
        kernel,
        grid=(depth,),
        in_specs=[
            pl.BlockSpec((stride, 2 * columns), lambda z: (0, z)),
            pl.BlockSpec((groups, 2 * columns), lambda z: (0, z)),
        ],
        out_specs=(pl.BlockSpec((stride, 2 * columns), lambda z: (0, z)), half, half),
        out_shape=(jax.ShapeDtypeStruct((stride, width), BF), halves, halves),
        cost_estimate=pl.CostEstimate(
            flops=2 * stride * width, bytes_accessed=6 * stride * width, transcendentals=0
        ),
        compiler_params=pltpu.CompilerParams(vmem_limit_bytes=32 * 1024 * 1024),
    )(codes, scales)


def pair_products(rotated, neighbour, own, other):
    depth, stride, columns = own.shape
    height = rotated.shape[0]
    step = 2

    def kernel(rotated_ref, neighbour_ref, own_ref, other_ref, out_ref):
        for z in range(step):
            total = dot(rotated_ref[...], own_ref[z]) + dot(neighbour_ref[...], other_ref[z])
            out_ref[z] = total

    rows = pl.BlockSpec((height, stride), lambda z: (0, 0))
    half = pl.BlockSpec((step, stride, columns), lambda z: (z, 0, 0))
    return pl.pallas_call(
        kernel,
        grid=(depth // step,),
        in_specs=[rows, rows, half, half],
        out_specs=pl.BlockSpec((step, height, columns), lambda z: (z, 0, 0)),
        out_shape=jax.ShapeDtypeStruct((depth, height, columns), F32),
        cost_estimate=pl.CostEstimate(
            flops=4 * height * stride * depth * columns,
            bytes_accessed=4 * depth * columns * (stride + height),
            transcendentals=0,
        ),
        compiler_params=pltpu.CompilerParams(vmem_limit_bytes=32 * 1024 * 1024),
    )(rotated, neighbour, own, other)


def to_chunks(values, signs):
    height, stride = values.shape
    halves = stride // LANES
    blocks = height // ROWS

    def kernel(values_ref, signs_ref, out_ref):
        sign = (2 * signs_ref[...] - 1).astype(F32)
        signed = (values_ref[...].astype(F32) * sign).astype(BF)
        place = placement(blocks, ROWS)
        for half in range(halves):
            part = dot(place, signed[:, half * LANES : (half + 1) * LANES])
            part = part.astype(BF).reshape(blocks, TILE, LANES)
            out_ref[half * blocks : (half + 1) * blocks] = part

    out = jax.ShapeDtypeStruct((halves * blocks, TILE, LANES), BF)
    return whole(kernel, out, values, signs.reshape(1, stride))


def hadamard(parts):
    step = 1
    while step < len(parts):
        for low in range(len(parts)):
            if low & step == 0:
                one, two = parts[low], parts[low + step]
                parts[low], parts[low + step] = one + two, one - two
        step *= 2
    return parts


def mix_blocks(chunks):
    def kernel(chunks_ref, out_ref, sum_ref):
        values = chunks_ref[...].astype(F32)
        mixed = hadamard([values[p] for p in range(values.shape[0])])
        row = lax.broadcasted_iota(jnp.int32, (TILE, LANES), 0)
        sum_ref[...] = mixed[0]
        for p, part in enumerate(mixed):
            out_ref[p] = jnp.where(row < ROWS, part, mixed[0]).astype(BF)

    out = jax.ShapeDtypeStruct(chunks.shape, BF), jax.ShapeDtypeStruct((TILE, LANES), F32)
    return whole(kernel, out, chunks)


def gather_rows(chunks, blocks):
    flat = chunks.reshape(-1, LANES)
    place = placement(blocks, ROWS)
    size = blocks * TILE
    halves = flat.shape[0] // size
    parts = [
        dot(place, flat[half * size : (half + 1) * size], ((0,), (0,))) for half in range(halves)
    ]
    return jnp.concatenate(parts, axis=1)


def finish_rotation(chunks, spread, scaling):
    blocks = chunks.shape[0] * LANES // spread.shape[0]

    def kernel(chunks_ref, spread_ref, out_ref):
        values = gather_rows(chunks_ref[...], blocks).astype(BF)
        out_ref[...] = (dot(values, spread_ref[...]) * scaling).astype(BF)

    out = jax.ShapeDtypeStruct((blocks * ROWS, spread.shape[0]), BF)
    return whole(kernel, out, chunks, spread)


def finish_gradient(chunks, signs):
    stride = signs.shape[0]
    blocks = chunks.shape[0] * LANES // stride

    def kernel(chunks_ref, signs_ref, out_ref):
        sign = (2 * signs_ref[...] - 1).astype(F32)
        out_ref[...] = (gather_rows(chunks_ref[...], blocks) * sign).astype(BF)

    out = jax.ShapeDtypeStruct((blocks * ROWS, stride), BF)
    return whole(kernel, out, chunks, signs.reshape(1, stride))


def backward_chunks(main, adapter_grad, down_map, rotated, spread, scaling):
    height, stride = main.shape
    halves = stride // LANES
    blocks = height // ROWS
    peers = halves * blocks
    rest = height - LANES

    def kernel(main_ref, grad_ref, down_ref, rotated_ref, spread_ref, out_ref):
        rotated_value = rotated_ref[...]
        down = down_ref[...]
        d_rotated = main_ref[...] + dot(grad_ref[...], down, ((1,), (1,)))
        local = dot(d_rotated.astype(BF), spread_ref[...])
        local = (local * scaling).astype(BF)
        product = rotated_value.astype(F32) * d_rotated
        totals = lax.dot_general(
            jnp.ones((TILE, stride), F32),
            product,
            (((1,), (1,)), ((), ())),
            precision=HIGH_ACCURACY,
            preferred_element_type=F32,
        )
        adapter = dot(down, rotated_value, ((0,), (1,))).astype(BF)
        pad = jnp.zeros((peers, LANES - rest), BF)
        riders = dot(rider_rows(peers, ROWS), adapter[:, :LANES])
        tail = jnp.concatenate([adapter[:, LANES:], pad], axis=1)
        riders += dot(rider_rows(peers, ROWS + 1), tail)
        row_tail = jnp.concatenate(
            [totals[:, LANES:], jnp.zeros((TILE, LANES - rest), F32)], axis=1
        )
        row_tail = pltpu.roll(row_tail, rest, 1)
        k = lax.broadcasted_iota(jnp.int32, (TILE, LANES), 0)
        extra = jnp.where(k == ROWS + 2, totals[:, :LANES], 0.0)
        extra += jnp.where(k == ROWS + 1, row_tail, 0.0)
        place = placement(blocks, ROWS)
        for half in range(halves):
            part = dot(place, local[:, half * LANES : (half + 1) * LANES])
            part += riders[half * blocks * TILE : (half + 1) * blocks * TILE]
            part = part.reshape(blocks, TILE, LANES) + extra[None]
            out_ref[half * blocks : (half + 1) * blocks] = part.astype(BF)

    out = jax.ShapeDtypeStruct((peers, TILE, LANES), BF)
    return whole(kernel, out, main, adapter_grad, down_map, rotated, spread)


def split(values):
    high = lax.reduce_precision(values, 8, 7)
    return high, lax.reduce_precision(values - high, 8, 7)


def body(
    hidden, codes, scales, signs, lowrank_down_map, lowrank_up_map, experts, gates, output_gradient
):
    slot_rows, stride = hidden.shape
    replicas, depth = lax.axis_size("r"), lax.axis_size("z")
    devices = EXPERT_COUNT * replicas
    rank = lowrank_down_map.shape[1]
    expert_position = lax.axis_index("e")
    replica = lax.axis_index("r")
    capacity = slot_rows // devices
    tokens_here = experts.shape[0]
    columns = output_gradient.shape[1]
    scaling = 1.0 / math.sqrt(HIDDEN_UNITS)

    row = np.arange(devices * capacity)
    row_slot = row // (replicas * capacity) * capacity + row % capacity
    row_slot = jnp.asarray(row_slot[None], jnp.int32)
    outgoing, target = route(experts, gates, output_gradient, row_slot, capacity)
    target = target.reshape(tokens_here * 2)
    weights, own, other = dequantize(codes, scales, depth, columns)
    d_rows = exchange(outgoing, EXPERT)
    chunks = to_chunks(hidden, signs)
    d_rows, weights, own, other, chunks = lax.optimization_barrier(
        (d_rows, weights, own, other, chunks)
    )
    lowrank_local = lax.dynamic_index_in_dim(lowrank_up_map, expert_position, 0, keepdims=False)
    gathered = lax.all_gather(
        jnp.concatenate([d_rows, lowrank_local], axis=0), TENSOR, axis=1, tiled=True
    )

    spread_local = sylvester(stride)
    mixed_blocks, _ = mix_blocks(exchange(chunks, SLAB))
    rotated = finish_rotation(exchange(mixed_blocks, SLAB), spread_local, scaling)

    other = lax.ppermute(other, "c", [(0, 1), (1, 0)])
    neighbour = lax.ppermute(rotated, "c", [(0, 1), (1, 0)])
    pair = pair_products(rotated, neighbour, own, other)
    frozen = lax.psum_scatter(pair, "z", scatter_dimension=0, tiled=False)

    d_full = gathered[:slot_rows]
    lowrank_full = gathered[slot_rows:]
    adapter_grad = LOWRANK_SCALE * lax.dot_general(
        d_full, lowrank_full, (((1,), (1,)), ((), ())), preferred_element_type=F32
    )
    adapter_grad = adapter_grad.astype(BF)
    main = dot(d_full, weights, ((1,), (1,)))
    down_map_gradient = dot(rotated, adapter_grad, ((0,), (0,)))
    d_chunks = exchange(
        backward_chunks(main, adapter_grad, lowrank_down_map, rotated, spread_local, scaling), SLAB
    )
    d_mixed, sums = mix_blocks(d_chunks)
    rest = slot_rows - LANES
    row_total = jnp.concatenate([sums[ROWS + 2], sums[ROWS + 1, rest : 2 * rest]])
    d_mixed = exchange(d_mixed, SLAB)
    hidden_gradient = finish_gradient(d_mixed, signs)
    adapter_in = jnp.concatenate([d_mixed[:, ROWS], d_mixed[:, ROWS + 1, :rest]], axis=1)

    slot_output = frozen + (LOWRANK_SCALE / replicas) * lax.dot_general(
        adapter_in, lowrank_local, (((0,), (0,)), ((), ())), preferred_element_type=F32
    )
    share = rank // replicas
    adapter_share = lax.dynamic_slice_in_dim(adapter_in, replica * share, share, 0)
    up_share = LOWRANK_SCALE * jnp.dot(adapter_share, d_rows, preferred_element_type=F32)
    totals = jnp.concatenate(
        [part.astype(BF).reshape(devices, capacity) for part in split(row_total)], axis=1
    )
    totals = jnp.pad(totals, ((0, 0), (0, columns - 2 * capacity)))[:, None, :]
    parcel = jnp.concatenate(
        [
            slot_output.astype(BF).reshape(devices, capacity, columns),
            totals,
            jnp.broadcast_to(up_share.astype(BF)[None], (devices, share, columns)),
        ],
        axis=1,
    )
    parcel = exchange(parcel, EXPERT)
    up_map_gradient = (
        parcel[:, capacity + 1 :].astype(F32).reshape(EXPERT_COUNT, rank, columns)
    )
    summed = (
        parcel[:, :capacity]
        .astype(F32)
        .reshape(EXPERT_COUNT, replicas, capacity, columns)
        .sum(axis=1)
        .reshape(EXPERT_COUNT * capacity, columns)
    )
    totals = parcel.reshape(EXPERT_COUNT, replicas, capacity + 1 + share, columns)[:, 0, capacity]
    totals = totals[:, : 2 * capacity].astype(F32)
    totals = (totals[:, :capacity] + totals[:, capacity:]).reshape(EXPERT_COUNT * capacity)
    slot_id = jnp.arange(EXPERT_COUNT * capacity, dtype=jnp.int32)
    chosen = target[:, None] == slot_id[None, :]
    gates_gradient = jnp.sum(jnp.where(chosen, totals[None, :], 0.0), axis=1)
    gates_gradient = gates_gradient.reshape(tokens_here, 2) / gates
    chosen = chosen.reshape(tokens_here, 2, EXPERT_COUNT * capacity)
    mixer = jnp.sum(jnp.where(chosen, gates[:, :, None], 0.0), axis=1)
    mixed = jnp.dot(mixer, summed, precision=HIGH_ACCURACY).astype(BF)
    return (mixed, hidden_gradient, down_map_gradient, up_map_gradient, gates_gradient)


def solution(mesh):
    owners, tensor = mesh.devices.shape
    split = Mesh(
        mesh.devices.reshape(EXPERT_COUNT, owners // EXPERT_COUNT, tensor // 2, 2),
        ("e", "r", "z", "c"),
    )
    every = EXPERT + TENSOR
    placed = (
        P(None, every),
        P(every, None),
        P(every, None),
        P(every),
        P(every, None),
        P(None, None, TENSOR),
        P(EXPERT, None),
        P(EXPERT, None),
        P(EXPERT, TENSOR),
    )
    return jax.shard_map(
        body,
        mesh=split,
        in_specs=placed,
        out_specs=(
            P(EXPERT, TENSOR),
            P(None, every),
            P(every, None),
            P(None, None, TENSOR),
            P(EXPERT, None),
        ),
        check_vma=False,
    )
```

```python
import math

import jax
import jax.numpy as jnp
import numpy as np
from jax import lax
from jax.experimental import pallas as pl
from jax.experimental.pallas import tpu as pltpu
from jax.sharding import Mesh
from jax.sharding import PartitionSpec as P

HIDDEN_UNITS = 16384
EXPERT_COUNT = 8
LOWRANK_SCALE = 0.5
HIGH_ACCURACY = lax.Precision.HIGHEST
BF = jnp.bfloat16
F32 = jnp.float32
EXPERT = ("e", "r")
TENSOR = ("z", "c")
SLAB = ("r", "z", "c")
LANES = 128
TILE = 8
ROWS = 5


def sylvester(count):
    table = np.ones((1, 1), np.float32)
    while table.shape[0] < count:
        table = np.kron(np.array([[1.0, 1.0], [1.0, -1.0]], np.float32), table)
    return jnp.asarray(table, BF)


def exchange(value, axes):
    return lax.all_to_all(value, axes, split_axis=0, concat_axis=0, tiled=True)


def dot(left, right, dims=((1,), (0,))):
    return lax.dot_general(left, right, (dims, ((), ())), preferred_element_type=F32)


def placement(blocks, rows):
    out_row = lax.broadcasted_iota(jnp.int32, (blocks * TILE, blocks * rows), 0)
    in_row = lax.broadcasted_iota(jnp.int32, (blocks * TILE, blocks * rows), 1)
    k = out_row % TILE
    return jnp.where((k < rows) & (out_row // TILE * rows + k == in_row), 1.0, 0.0).astype(BF)


def rider_rows(peers, k):
    out_row = lax.broadcasted_iota(jnp.int32, (peers * TILE, peers), 0)
    in_row = lax.broadcasted_iota(jnp.int32, (peers * TILE, peers), 1)
    return jnp.where(out_row == in_row * TILE + k, 1.0, 0.0).astype(BF)


def whole(kernel, out_shape, *operands):
    return pl.pallas_call(
        kernel,
        out_shape=out_shape,
        compiler_params=pltpu.CompilerParams(vmem_limit_bytes=32 * 1024 * 1024),
    )(*operands)


def route(experts, gates, output_gradient, replicas, capacity):
    choices, tokens = experts.shape
    columns = output_gradient.shape[1]
    devices = EXPERT_COUNT * replicas

    def kernel(experts_ref, gates_ref, grad_ref, out_ref, target_ref):
        ids = experts_ref[...]
        gate = gates_ref[...]
        expert = lax.broadcasted_iota(jnp.int32, (EXPERT_COUNT, tokens), 0)
        named = [
            jnp.where(ids[k : k + 1] == expert, 1.0, 0.0) for k in range(choices)
        ]
        row = lax.broadcasted_iota(jnp.int32, (tokens, tokens), 0)
        col = lax.broadcasted_iota(jnp.int32, (tokens, tokens), 1)
        upper = jnp.where(row < col, 1.0, 0.0).astype(BF)
        earlier = dot(sum(named).astype(BF), upper)
        place = lax.broadcasted_iota(jnp.int32, (devices * TILE, tokens), 0)
        k_row = place % TILE
        slot_row = place // (replicas * TILE) * capacity + k_row
        picked = jnp.zeros((devices * TILE, tokens), F32)
        weight = jnp.zeros((devices * TILE, tokens), F32)
        targets = []
        for k in range(choices):
            slot = jnp.sum(earlier * named[k], axis=0, keepdims=True).astype(jnp.int32)
            target = ids[k : k + 1] * capacity + slot
            match = jnp.where((target == slot_row) & (k_row < capacity), 1.0, 0.0)
            picked = picked + match
            weight = weight + match * gate[k : k + 1]
            earlier = earlier + named[k]
            targets.append(target)
        values = dot(picked.astype(BF), grad_ref[...])
        values = values * jnp.sum(weight, axis=1, keepdims=True)
        values = values.reshape(devices, TILE, columns)[:, :capacity]
        out_ref[...] = values.astype(BF)
        choice = lax.broadcasted_iota(jnp.int32, (choices, tokens), 0)
        chosen = jnp.broadcast_to(targets[0], (choices, tokens))
        for k in range(1, choices):
            chosen = jnp.where(choice == k, targets[k], chosen)
        target_ref[...] = chosen

    out = (
        jax.ShapeDtypeStruct((devices, capacity, columns), BF),
        jax.ShapeDtypeStruct((choices, tokens), jnp.int32),
    )
    return whole(kernel, out, experts, gates, output_gradient)


def dequantize(codes, scales, depth, columns):
    stride, width = codes.shape
    groups = scales.shape[0]
    size = stride // groups

    def kernel(codes_ref, scales_ref, all_ref, own_ref, other_ref):
        first = lax.axis_index("c") == 0
        for group in range(groups):
            rows = slice(group * size, (group + 1) * size)
            values = codes_ref[rows, :].astype(F32) * scales_ref[group : group + 1, :]
            all_ref[rows, :] = values.astype(BF)
            low, high = values[:, :columns], values[:, columns:]
            own_ref[0, rows, :] = jnp.where(first, low, high).astype(BF)
            other_ref[0, rows, :] = jnp.where(first, high, low).astype(BF)

    half = pl.BlockSpec((1, stride, columns), lambda z: (z, 0, 0))
    halves = jax.ShapeDtypeStruct((depth, stride, columns), BF)
    return pl.pallas_call(
        kernel,
        grid=(depth,),
        in_specs=[
            pl.BlockSpec((stride, 2 * columns), lambda z: (0, z)),
            pl.BlockSpec((groups, 2 * columns), lambda z: (0, z)),
        ],
        out_specs=(pl.BlockSpec((stride, 2 * columns), lambda z: (0, z)), half, half),
        out_shape=(jax.ShapeDtypeStruct((stride, width), BF), halves, halves),
        cost_estimate=pl.CostEstimate(
            flops=2 * stride * width, bytes_accessed=6 * stride * width, transcendentals=0
        ),
        compiler_params=pltpu.CompilerParams(vmem_limit_bytes=32 * 1024 * 1024),
    )(codes, scales)


def pair_products(rotated, neighbour, own, other):
    depth, stride, columns = own.shape
    height = rotated.shape[0]
    step = 2

    def kernel(rotated_ref, neighbour_ref, own_ref, other_ref, out_ref):
        for z in range(step):
            total = dot(rotated_ref[...], own_ref[z]) + dot(neighbour_ref[...], other_ref[z])
            out_ref[z] = total

    rows = pl.BlockSpec((height, stride), lambda z: (0, 0))
    half = pl.BlockSpec((step, stride, columns), lambda z: (z, 0, 0))
    return pl.pallas_call(
        kernel,
        grid=(depth // step,),
        in_specs=[rows, rows, half, half],
        out_specs=pl.BlockSpec((step, height, columns), lambda z: (z, 0, 0)),
        out_shape=jax.ShapeDtypeStruct((depth, height, columns), F32),
        cost_estimate=pl.CostEstimate(
            flops=4 * height * stride * depth * columns,
            bytes_accessed=4 * depth * columns * (stride + height),
            transcendentals=0,
        ),
        compiler_params=pltpu.CompilerParams(vmem_limit_bytes=32 * 1024 * 1024),
    )(rotated, neighbour, own, other)


def to_chunks(values, signs):
    height, stride = values.shape
    halves = stride // LANES
    blocks = height // ROWS

    def kernel(values_ref, signs_ref, out_ref):
        sign = (2 * signs_ref[...] - 1).astype(F32)
        signed = (values_ref[...].astype(F32) * sign).astype(BF)
        place = placement(blocks, ROWS)
        for half in range(halves):
            part = dot(place, signed[:, half * LANES : (half + 1) * LANES])
            part = part.astype(BF).reshape(blocks, TILE, LANES)
            out_ref[half * blocks : (half + 1) * blocks] = part

    out = jax.ShapeDtypeStruct((halves * blocks, TILE, LANES), BF)
    return whole(kernel, out, values, signs.reshape(1, stride))


def hadamard(parts):
    step = 1
    while step < len(parts):
        for low in range(len(parts)):
            if low & step == 0:
                one, two = parts[low], parts[low + step]
                parts[low], parts[low + step] = one + two, one - two
        step *= 2
    return parts


def mix_blocks(chunks):
    def kernel(chunks_ref, out_ref, sum_ref):
        values = chunks_ref[...].astype(F32)
        mixed = hadamard([values[p] for p in range(values.shape[0])])
        row = lax.broadcasted_iota(jnp.int32, (TILE, LANES), 0)
        sum_ref[...] = mixed[0]
        for p, part in enumerate(mixed):
            out_ref[p] = jnp.where(row < ROWS, part, mixed[0]).astype(BF)

    out = jax.ShapeDtypeStruct(chunks.shape, BF), jax.ShapeDtypeStruct((TILE, LANES), F32)
    return whole(kernel, out, chunks)


def gather_rows(chunks, blocks):
    flat = chunks.reshape(-1, LANES)
    place = placement(blocks, ROWS)
    size = blocks * TILE
    halves = flat.shape[0] // size
    parts = [
        dot(place, flat[half * size : (half + 1) * size], ((0,), (0,))) for half in range(halves)
    ]
    return jnp.concatenate(parts, axis=1)


def finish_rotation(chunks, spread, scaling):
    blocks = chunks.shape[0] * LANES // spread.shape[0]

    def kernel(chunks_ref, spread_ref, out_ref):
        values = gather_rows(chunks_ref[...], blocks).astype(BF)
        out_ref[...] = (dot(values, spread_ref[...]) * scaling).astype(BF)

    out = jax.ShapeDtypeStruct((blocks * ROWS, spread.shape[0]), BF)
    return whole(kernel, out, chunks, spread)


def finish_gradient(chunks, signs):
    stride = signs.shape[0]
    blocks = chunks.shape[0] * LANES // stride

    def kernel(chunks_ref, signs_ref, out_ref):
        sign = (2 * signs_ref[...] - 1).astype(F32)
        out_ref[...] = (gather_rows(chunks_ref[...], blocks) * sign).astype(BF)

    out = jax.ShapeDtypeStruct((blocks * ROWS, stride), BF)
    return whole(kernel, out, chunks, signs.reshape(1, stride))


def backward_chunks(gathered, weights, down_map, rotated, spread, scaling):
    height, stride = rotated.shape
    rank = down_map.shape[1]
    width = weights.shape[1]
    halves = stride // LANES
    blocks = height // ROWS
    peers = halves * blocks
    rest = height - LANES
    steps = 4
    block = width // steps

    def kernel(
        gathered_ref, weights_ref, down_ref, rotated_ref, spread_ref, out_ref, grad_ref, acc, small
    ):
        @pl.when(pl.program_id(0) == 0)
        def _():
            acc[...] = jnp.zeros_like(acc)
            small[...] = jnp.zeros_like(small)

        slots = gathered_ref[:height, :]
        acc[...] += dot(slots, weights_ref[...], ((1,), (1,)))
        small[...] += dot(slots, gathered_ref[height:, :], ((1,), (1,)))

        @pl.when(pl.program_id(0) == steps - 1)
        def _():
            rotated_value = rotated_ref[...]
            down = down_ref[...]
            adapter_grad = (LOWRANK_SCALE * small[...]).astype(BF)
            grad_ref[...] = adapter_grad
            d_rotated = acc[...] + dot(adapter_grad, down, ((1,), (1,)))
            local = dot(d_rotated.astype(BF), spread_ref[...])
            local = (local * scaling).astype(BF)
            product = rotated_value.astype(F32) * d_rotated
            totals = lax.dot_general(
                jnp.ones((TILE, stride), F32),
                product,
                (((1,), (1,)), ((), ())),
                precision=HIGH_ACCURACY,
                preferred_element_type=F32,
            )
            adapter = dot(down, rotated_value, ((0,), (1,))).astype(BF)
            pad = jnp.zeros((peers, LANES - rest), BF)
            riders = dot(rider_rows(peers, ROWS), adapter[:, :LANES])
            tail = jnp.concatenate([adapter[:, LANES:], pad], axis=1)
            riders += dot(rider_rows(peers, ROWS + 1), tail)
            row_tail = jnp.concatenate(
                [totals[:, LANES:], jnp.zeros((TILE, LANES - rest), F32)], axis=1
            )
            row_tail = pltpu.roll(row_tail, rest, 1)
            k = lax.broadcasted_iota(jnp.int32, (TILE, LANES), 0)
            extra = jnp.where(k == ROWS + 2, totals[:, :LANES], 0.0)
            extra += jnp.where(k == ROWS + 1, row_tail, 0.0)
            place = placement(blocks, ROWS)
            for half in range(halves):
                part = dot(place, local[:, half * LANES : (half + 1) * LANES])
                part += riders[half * blocks * TILE : (half + 1) * blocks * TILE]
                part = part.reshape(blocks, TILE, LANES) + extra[None]
                out_ref[half * blocks : (half + 1) * blocks] = part.astype(BF)

    def fixed(shape):
        return pl.BlockSpec(shape, lambda i: (0,) * len(shape))

    return pl.pallas_call(
        kernel,
        grid=(steps,),
        in_specs=[
            pl.BlockSpec((height + rank, block), lambda i: (0, i)),
            pl.BlockSpec((stride, block), lambda i: (0, i)),
            fixed(down_map.shape),
            fixed(rotated.shape),
            fixed(spread.shape),
        ],
        out_specs=(fixed((peers, TILE, LANES)), fixed((height, rank))),
        out_shape=(
            jax.ShapeDtypeStruct((peers, TILE, LANES), BF),
            jax.ShapeDtypeStruct((height, rank), BF),
        ),
        scratch_shapes=[pltpu.VMEM((height, stride), F32), pltpu.VMEM((height, rank), F32)],
        cost_estimate=pl.CostEstimate(
            flops=2 * height * stride * width,
            bytes_accessed=2 * width * (stride + height + rank),
            transcendentals=0,
        ),
        compiler_params=pltpu.CompilerParams(vmem_limit_bytes=32 * 1024 * 1024),
    )(gathered, weights, down_map, rotated, spread)


def split(values):
    high = lax.reduce_precision(values, 8, 7)
    return high, lax.reduce_precision(values - high, 8, 7)


def body(
    hidden, codes, scales, signs, lowrank_down_map, lowrank_up_map, experts, gates, output_gradient
):
    slot_rows, stride = hidden.shape
    replicas, depth = lax.axis_size("r"), lax.axis_size("z")
    devices = EXPERT_COUNT * replicas
    rank = lowrank_down_map.shape[1]
    expert_position = lax.axis_index("e")
    replica = lax.axis_index("r")
    capacity = slot_rows // devices
    tokens_here = experts.shape[0]
    columns = output_gradient.shape[1]
    scaling = 1.0 / math.sqrt(HIDDEN_UNITS)

    outgoing, target = route(experts.T, gates.T, output_gradient, replicas, capacity)
    target = target.T.reshape(tokens_here * 2)
    weights, own, other = dequantize(codes, scales, depth, columns)
    d_rows = exchange(outgoing, EXPERT).reshape(slot_rows, columns)
    chunks = to_chunks(hidden, signs)
    d_rows, weights, own, other, chunks = lax.optimization_barrier(
        (d_rows, weights, own, other, chunks)
    )
    lowrank_local = lax.dynamic_index_in_dim(lowrank_up_map, expert_position, 0, keepdims=False)
    gathered = lax.all_gather(
        jnp.concatenate([d_rows, lowrank_local], axis=0), TENSOR, axis=1, tiled=True
    )

    spread_local = sylvester(stride)
    mixed_blocks, _ = mix_blocks(exchange(chunks, SLAB))
    rotated = finish_rotation(exchange(mixed_blocks, SLAB), spread_local, scaling)

    other = lax.ppermute(other, "c", [(0, 1), (1, 0)])
    neighbour = lax.ppermute(rotated, "c", [(0, 1), (1, 0)])
    pair = pair_products(rotated, neighbour, own, other)
    frozen = lax.psum_scatter(pair, "z", scatter_dimension=0, tiled=False)

    d_chunks, adapter_grad = backward_chunks(
        gathered, weights, lowrank_down_map, rotated, spread_local, scaling
    )
    down_map_gradient = dot(rotated, adapter_grad, ((0,), (0,)))
    d_chunks = exchange(d_chunks, SLAB)
    d_mixed, sums = mix_blocks(d_chunks)
    rest = slot_rows - LANES
    row_total = jnp.concatenate([sums[ROWS + 2], sums[ROWS + 1, rest : 2 * rest]])
    d_mixed = exchange(d_mixed, SLAB)
    hidden_gradient = finish_gradient(d_mixed, signs)
    adapter_in = jnp.concatenate([d_mixed[:, ROWS], d_mixed[:, ROWS + 1, :rest]], axis=1)

    slot_output = frozen + (LOWRANK_SCALE / replicas) * lax.dot_general(
        adapter_in, lowrank_local, (((0,), (0,)), ((), ())), preferred_element_type=F32
    )
    share = rank // replicas
    adapter_share = lax.dynamic_slice_in_dim(adapter_in, replica * share, share, 0)
    up_share = LOWRANK_SCALE * jnp.dot(adapter_share, d_rows, preferred_element_type=F32)
    totals = jnp.concatenate(
        [part.astype(BF).reshape(devices, capacity) for part in split(row_total)], axis=1
    )
    totals = jnp.pad(totals, ((0, 0), (0, columns - 2 * capacity)))[:, None, :]
    parcel = jnp.concatenate(
        [
            slot_output.astype(BF).reshape(devices, capacity, columns),
            totals,
            jnp.broadcast_to(up_share.astype(BF)[None], (devices, share, columns)),
        ],
        axis=1,
    )
    parcel = exchange(parcel, EXPERT)
    up_map_gradient = (
        parcel[:, capacity + 1 :].astype(F32).reshape(EXPERT_COUNT, rank, columns)
    )
    summed = (
        parcel[:, :capacity]
        .astype(F32)
        .reshape(EXPERT_COUNT, replicas, capacity, columns)
        .sum(axis=1)
        .reshape(EXPERT_COUNT * capacity, columns)
    )
    totals = parcel.reshape(EXPERT_COUNT, replicas, capacity + 1 + share, columns)[:, 0, capacity]
    totals = totals[:, : 2 * capacity].astype(F32)
    totals = (totals[:, :capacity] + totals[:, capacity:]).reshape(EXPERT_COUNT * capacity)
    slot_id = jnp.arange(EXPERT_COUNT * capacity, dtype=jnp.int32)
    chosen = target[:, None] == slot_id[None, :]
    gates_gradient = jnp.sum(jnp.where(chosen, totals[None, :], 0.0), axis=1)
    gates_gradient = gates_gradient.reshape(tokens_here, 2) / gates
    chosen = chosen.reshape(tokens_here, 2, EXPERT_COUNT * capacity)
    mixer = jnp.sum(jnp.where(chosen, gates[:, :, None], 0.0), axis=1)
    mixed = jnp.dot(mixer, summed, precision=HIGH_ACCURACY).astype(BF)
    return (mixed, hidden_gradient, down_map_gradient, up_map_gradient, gates_gradient)


def solution(mesh):
    owners, tensor = mesh.devices.shape
    split = Mesh(
        mesh.devices.reshape(EXPERT_COUNT, owners // EXPERT_COUNT, tensor // 2, 2),
        ("e", "r", "z", "c"),
    )
    every = EXPERT + TENSOR
    placed = (
        P(None, every),
        P(every, None),
        P(every, None),
        P(every),
        P(every, None),
        P(None, None, TENSOR),
        P(EXPERT, None),
        P(EXPERT, None),
        P(EXPERT, TENSOR),
    )
    return jax.shard_map(
        body,
        mesh=split,
        in_specs=placed,
        out_specs=(
            P(EXPERT, TENSOR),
            P(None, every),
            P(every, None),
            P(None, None, TENSOR),
            P(EXPERT, None),
        ),
        check_vma=False,
    )
```

```python
import math

import jax
import jax.numpy as jnp
import numpy as np
from jax import lax
from jax.experimental import pallas as pl
from jax.experimental.pallas import tpu as pltpu
from jax.sharding import Mesh
from jax.sharding import PartitionSpec as P

HIDDEN_UNITS = 16384
EXPERT_COUNT = 8
LOWRANK_SCALE = 0.5
HIGH_ACCURACY = lax.Precision.HIGHEST
BF = jnp.bfloat16
F32 = jnp.float32
EXPERT = ("e", "r")
TENSOR = ("z", "c")
SLAB = ("r", "z", "c")
LANES = 128
TILE = 8
ROWS = 5


def sylvester(count):
    table = np.ones((1, 1), np.float32)
    while table.shape[0] < count:
        table = np.kron(np.array([[1.0, 1.0], [1.0, -1.0]], np.float32), table)
    return jnp.asarray(table, BF)


def exchange(value, axes):
    return lax.all_to_all(value, axes, split_axis=0, concat_axis=0, tiled=True)


def dot(left, right, dims=((1,), (0,))):
    return lax.dot_general(left, right, (dims, ((), ())), preferred_element_type=F32)


def placement(blocks, rows):
    out_row = lax.broadcasted_iota(jnp.int32, (blocks * TILE, blocks * rows), 0)
    in_row = lax.broadcasted_iota(jnp.int32, (blocks * TILE, blocks * rows), 1)
    k = out_row % TILE
    return jnp.where((k < rows) & (out_row // TILE * rows + k == in_row), 1.0, 0.0).astype(BF)


def rider_rows(peers, k):
    out_row = lax.broadcasted_iota(jnp.int32, (peers * TILE, peers), 0)
    in_row = lax.broadcasted_iota(jnp.int32, (peers * TILE, peers), 1)
    return jnp.where(out_row == in_row * TILE + k, 1.0, 0.0).astype(BF)


def whole(kernel, out_shape, *operands):
    return pl.pallas_call(
        kernel,
        out_shape=out_shape,
        compiler_params=pltpu.CompilerParams(vmem_limit_bytes=32 * 1024 * 1024),
    )(*operands)


def route(experts, gates, output_gradient, replicas, capacity):
    choices, tokens = experts.shape
    columns = output_gradient.shape[1]
    rows = EXPERT_COUNT * replicas * capacity

    def kernel(experts_ref, gates_ref, grad_ref, out_ref, target_ref):
        ids = experts_ref[...]
        gate = gates_ref[...]
        expert = lax.broadcasted_iota(jnp.int32, (EXPERT_COUNT, tokens), 0)
        named = [
            jnp.where(ids[k : k + 1] == expert, 1.0, 0.0) for k in range(choices)
        ]
        row = lax.broadcasted_iota(jnp.int32, (tokens, tokens), 0)
        col = lax.broadcasted_iota(jnp.int32, (tokens, tokens), 1)
        upper = jnp.where(row < col, 1.0, 0.0).astype(BF)
        earlier = dot(sum(named).astype(BF), upper)
        place = lax.broadcasted_iota(jnp.int32, (rows, tokens), 0).astype(F32)
        block = jnp.floor((place + 0.5) * (1.0 / capacity))
        owner = jnp.floor((place + 0.5) * (1.0 / (replicas * capacity)))
        slot_row = (place + capacity * (owner - block)).astype(jnp.int32)
        picked = jnp.zeros((rows, tokens), F32)
        weight = jnp.zeros((rows, tokens), F32)
        targets = []
        for k in range(choices):
            slot = jnp.sum(earlier * named[k], axis=0, keepdims=True).astype(jnp.int32)
            target = ids[k : k + 1] * capacity + slot
            match = jnp.where(target == slot_row, 1.0, 0.0)
            picked = picked + match
            weight = weight + match * gate[k : k + 1]
            earlier = earlier + named[k]
            targets.append(target)
        values = dot(picked.astype(BF), grad_ref[...])
        out_ref[...] = (values * jnp.sum(weight, axis=1, keepdims=True)).astype(BF)
        choice = lax.broadcasted_iota(jnp.int32, (choices, tokens), 0)
        chosen = jnp.broadcast_to(targets[0], (choices, tokens))
        for k in range(1, choices):
            chosen = jnp.where(choice == k, targets[k], chosen)
        target_ref[...] = chosen

    out = (
        jax.ShapeDtypeStruct((rows, columns), BF),
        jax.ShapeDtypeStruct((choices, tokens), jnp.int32),
    )
    return whole(kernel, out, experts, gates, output_gradient)


def build_parcel(frozen, d_mixed, up_map, d_rows, totals):
    height, columns = frozen.shape
    devices = totals.shape[0]
    rank = up_map.shape[0]
    peers = d_mixed.shape[0]
    rest = height - LANES

    def kernel(frozen_ref, mixed_ref, up_ref, rows_ref, totals_ref, out_ref):
        flat = mixed_ref[...].reshape(peers * TILE, LANES)
        first = dot(rider_rows(peers, ROWS), flat, ((0,), (0,)))
        second = dot(rider_rows(peers, ROWS + 1), flat, ((0,), (0,)))
        adapter = jnp.concatenate([first, second[:, :rest]], axis=1).astype(BF)
        replicas = devices // EXPERT_COUNT
        share = rank // replicas
        slots = frozen_ref[...] + (LOWRANK_SCALE / replicas) * dot(
            adapter, up_ref[...], ((0,), (0,))
        )
        row = lax.broadcasted_iota(jnp.int32, (share, rank), 0)
        col = lax.broadcasted_iota(jnp.int32, (share, rank), 1)
        chosen = jnp.where(col == row + lax.axis_index("r") * share, 1.0, 0.0).astype(BF)
        part = dot(chosen, adapter).astype(BF)
        up = (LOWRANK_SCALE * dot(part, rows_ref[...])).astype(BF)
        out_ref[:, :share, :] = jnp.broadcast_to(up[None], (devices, share, columns))
        rows = dot(placement(devices, ROWS), slots.astype(BF))
        rows += dot(rider_rows(devices, ROWS), totals_ref[...])
        rows = rows.reshape(devices, TILE, columns)[:, : ROWS + 1]
        out_ref[:, share:, :] = rows.astype(BF)

    share = rank * EXPERT_COUNT // devices
    out = jax.ShapeDtypeStruct((devices, share + ROWS + 1, columns), BF)
    return whole(kernel, out, frozen, d_mixed, up_map, d_rows, totals)


def open_parcel(parcel, experts, gates, target, rank):
    devices, height, columns = parcel.shape
    choices, tokens = experts.shape
    replicas = devices // EXPERT_COUNT
    share = rank // replicas

    def kernel(parcel_ref, experts_ref, gates_ref, target_ref, mixed_ref, up_ref, grad_ref):
        values = parcel_ref[...].astype(F32)
        up_ref[...] = values[:, :share].reshape(EXPERT_COUNT, rank, columns)
        rest = values[:, share:].reshape(EXPERT_COUNT, replicas, ROWS + 1, columns).sum(axis=1)
        gate = gates_ref[...]
        target = target_ref[...]
        slot = target - experts_ref[...] * ROWS
        c = lax.broadcasted_iota(jnp.int32, (ROWS + 1, tokens), 0)
        mixed = jnp.zeros((tokens, columns), F32)
        for e in range(EXPERT_COUNT):
            mixer = jnp.zeros((ROWS + 1, tokens), F32)
            for k in range(choices):
                hit = (target[k : k + 1] == e * ROWS + c) & (c < ROWS)
                mixer = mixer + jnp.where(hit, gate[k : k + 1], 0.0)
            mixed = mixed + lax.dot_general(
                mixer,
                rest[e],
                (((0,), (0,)), ((), ())),
                precision=HIGH_ACCURACY,
                preferred_element_type=F32,
            )
        mixed_ref[...] = mixed.astype(BF)
        totals = jnp.concatenate(
            [rest[e, ROWS : ROWS + 1, :LANES] for e in range(EXPERT_COUNT)], axis=0
        )
        totals = (totals * (1.0 / replicas)).astype(BF)
        expert = lax.broadcasted_iota(jnp.int32, (EXPERT_COUNT, tokens), 0)
        lane = lax.broadcasted_iota(jnp.int32, (LANES, tokens), 0)
        grads = []
        for k in range(choices):
            named = jnp.where(experts_ref[k : k + 1, :] == expert, 1.0, 0.0).astype(BF)
            by_lane = dot(totals, named, ((0,), (0,)))
            at = slot[k : k + 1]
            hit = (lane == at) | (lane == at + ROWS)
            grads.append(jnp.sum(jnp.where(hit, by_lane, 0.0), axis=0, keepdims=True))
        grad_ref[...] = jnp.concatenate(grads, axis=0) / gate

    out = (
        jax.ShapeDtypeStruct((tokens, columns), BF),
        jax.ShapeDtypeStruct((EXPERT_COUNT, rank, columns), F32),
        jax.ShapeDtypeStruct((choices, tokens), F32),
    )
    return whole(kernel, out, parcel, experts, gates, target)


def dequantize(codes, scales, depth, columns):
    stride, width = codes.shape
    groups = scales.shape[0]
    size = stride // groups

    def kernel(codes_ref, scales_ref, all_ref, own_ref, other_ref):
        first = lax.axis_index("c") == 0
        for group in range(groups):
            rows = slice(group * size, (group + 1) * size)
            values = codes_ref[rows, :].astype(F32) * scales_ref[group : group + 1, :]
            all_ref[rows, :] = values.astype(BF)
            low, high = values[:, :columns], values[:, columns:]
            own_ref[0, rows, :] = jnp.where(first, low, high).astype(BF)
            other_ref[0, rows, :] = jnp.where(first, high, low).astype(BF)

    half = pl.BlockSpec((1, stride, columns), lambda z: (z, 0, 0))
    halves = jax.ShapeDtypeStruct((depth, stride, columns), BF)
    return pl.pallas_call(
        kernel,
        grid=(depth,),
        in_specs=[
            pl.BlockSpec((stride, 2 * columns), lambda z: (0, z)),
            pl.BlockSpec((groups, 2 * columns), lambda z: (0, z)),
        ],
        out_specs=(pl.BlockSpec((stride, 2 * columns), lambda z: (0, z)), half, half),
        out_shape=(jax.ShapeDtypeStruct((stride, width), BF), halves, halves),
        cost_estimate=pl.CostEstimate(
            flops=2 * stride * width, bytes_accessed=6 * stride * width, transcendentals=0
        ),
        compiler_params=pltpu.CompilerParams(vmem_limit_bytes=32 * 1024 * 1024),
    )(codes, scales)


def pair_products(rotated, neighbour, own, other):
    depth, stride, columns = own.shape
    height = rotated.shape[0]
    step = 2

    def kernel(rotated_ref, neighbour_ref, own_ref, other_ref, out_ref):
        for z in range(step):
            total = dot(rotated_ref[...], own_ref[z]) + dot(neighbour_ref[...], other_ref[z])
            out_ref[z] = total

    rows = pl.BlockSpec((height, stride), lambda z: (0, 0))
    half = pl.BlockSpec((step, stride, columns), lambda z: (z, 0, 0))
    return pl.pallas_call(
        kernel,
        grid=(depth // step,),
        in_specs=[rows, rows, half, half],
        out_specs=pl.BlockSpec((step, height, columns), lambda z: (z, 0, 0)),
        out_shape=jax.ShapeDtypeStruct((depth, height, columns), F32),
        cost_estimate=pl.CostEstimate(
            flops=4 * height * stride * depth * columns,
            bytes_accessed=4 * depth * columns * (stride + height),
            transcendentals=0,
        ),
        compiler_params=pltpu.CompilerParams(vmem_limit_bytes=32 * 1024 * 1024),
    )(rotated, neighbour, own, other)


def to_chunks(values, signs):
    height, stride = values.shape
    halves = stride // LANES
    blocks = height // ROWS

    def kernel(values_ref, signs_ref, out_ref):
        sign = (2 * signs_ref[...] - 1).astype(F32)
        signed = (values_ref[...].astype(F32) * sign).astype(BF)
        place = placement(blocks, ROWS)
        for half in range(halves):
            part = dot(place, signed[:, half * LANES : (half + 1) * LANES])
            part = part.astype(BF).reshape(blocks, TILE, LANES)
            out_ref[half * blocks : (half + 1) * blocks] = part

    out = jax.ShapeDtypeStruct((halves * blocks, TILE, LANES), BF)
    return whole(kernel, out, values, signs.reshape(1, stride))


def hadamard(parts):
    step = 1
    while step < len(parts):
        for low in range(len(parts)):
            if low & step == 0:
                one, two = parts[low], parts[low + step]
                parts[low], parts[low + step] = one + two, one - two
        step *= 2
    return parts


def mix_blocks(chunks):
    def kernel(chunks_ref, out_ref, sum_ref):
        values = chunks_ref[...].astype(F32)
        mixed = hadamard([values[p] for p in range(values.shape[0])])
        row = lax.broadcasted_iota(jnp.int32, (TILE, LANES), 0)
        sum_ref[...] = mixed[0]
        for p, part in enumerate(mixed):
            out_ref[p] = jnp.where(row < ROWS, part, mixed[0]).astype(BF)

    out = jax.ShapeDtypeStruct(chunks.shape, BF), jax.ShapeDtypeStruct((TILE, LANES), F32)
    return whole(kernel, out, chunks)


def gather_rows(chunks, blocks):
    flat = chunks.reshape(-1, LANES)
    place = placement(blocks, ROWS)
    size = blocks * TILE
    halves = flat.shape[0] // size
    parts = [
        dot(place, flat[half * size : (half + 1) * size], ((0,), (0,))) for half in range(halves)
    ]
    return jnp.concatenate(parts, axis=1)


def finish_rotation(chunks, spread, scaling):
    blocks = chunks.shape[0] * LANES // spread.shape[0]

    def kernel(chunks_ref, spread_ref, out_ref):
        values = gather_rows(chunks_ref[...], blocks).astype(BF)
        out_ref[...] = (dot(values, spread_ref[...]) * scaling).astype(BF)

    out = jax.ShapeDtypeStruct((blocks * ROWS, spread.shape[0]), BF)
    return whole(kernel, out, chunks, spread)


def finish_gradient(chunks, signs):
    stride = signs.shape[0]
    blocks = chunks.shape[0] * LANES // stride

    def kernel(chunks_ref, signs_ref, out_ref):
        sign = (2 * signs_ref[...] - 1).astype(F32)
        out_ref[...] = (gather_rows(chunks_ref[...], blocks) * sign).astype(BF)

    out = jax.ShapeDtypeStruct((blocks * ROWS, stride), BF)
    return whole(kernel, out, chunks, signs.reshape(1, stride))


def backward_chunks(main, adapter_grad, down_map, rotated, spread, scaling):
    height, stride = main.shape
    halves = stride // LANES
    blocks = height // ROWS
    peers = halves * blocks
    rest = height - LANES

    def kernel(main_ref, grad_ref, down_ref, rotated_ref, spread_ref, out_ref):
        rotated_value = rotated_ref[...]
        down = down_ref[...]
        d_rotated = main_ref[...] + dot(grad_ref[...], down, ((1,), (1,)))
        local = dot(d_rotated.astype(BF), spread_ref[...])
        local = (local * scaling).astype(BF)
        product = rotated_value.astype(F32) * d_rotated
        totals = lax.dot_general(
            jnp.ones((TILE, stride), F32),
            product,
            (((1,), (1,)), ((), ())),
            precision=HIGH_ACCURACY,
            preferred_element_type=F32,
        )
        adapter = dot(down, rotated_value, ((0,), (1,))).astype(BF)
        pad = jnp.zeros((peers, LANES - rest), BF)
        riders = dot(rider_rows(peers, ROWS), adapter[:, :LANES])
        tail = jnp.concatenate([adapter[:, LANES:], pad], axis=1)
        riders += dot(rider_rows(peers, ROWS + 1), tail)
        row_tail = jnp.concatenate(
            [totals[:, LANES:], jnp.zeros((TILE, LANES - rest), F32)], axis=1
        )
        row_tail = pltpu.roll(row_tail, rest, 1)
        k = lax.broadcasted_iota(jnp.int32, (TILE, LANES), 0)
        extra = jnp.where(k == ROWS + 2, totals[:, :LANES], 0.0)
        extra += jnp.where(k == ROWS + 1, row_tail, 0.0)
        place = placement(blocks, ROWS)
        for half in range(halves):
            part = dot(place, local[:, half * LANES : (half + 1) * LANES])
            part += riders[half * blocks * TILE : (half + 1) * blocks * TILE]
            part = part.reshape(blocks, TILE, LANES) + extra[None]
            out_ref[half * blocks : (half + 1) * blocks] = part.astype(BF)

    out = jax.ShapeDtypeStruct((peers, TILE, LANES), BF)
    return whole(kernel, out, main, adapter_grad, down_map, rotated, spread)


def split(values):
    high = lax.reduce_precision(values, 8, 7)
    return high, lax.reduce_precision(values - high, 8, 7)


def body(
    hidden, codes, scales, signs, lowrank_down_map, lowrank_up_map, experts, gates, output_gradient
):
    slot_rows, stride = hidden.shape
    replicas, depth = lax.axis_size("r"), lax.axis_size("z")
    devices = EXPERT_COUNT * replicas
    rank = lowrank_down_map.shape[1]
    expert_position = lax.axis_index("e")
    capacity = slot_rows // devices
    columns = output_gradient.shape[1]
    scaling = 1.0 / math.sqrt(HIDDEN_UNITS)

    outgoing, target = route(experts.T, gates.T, output_gradient, replicas, capacity)
    weights, own, other = dequantize(codes, scales, depth, columns)
    d_rows = exchange(outgoing, EXPERT)
    chunks = to_chunks(hidden, signs)
    d_rows, weights, own, other, chunks = lax.optimization_barrier(
        (d_rows, weights, own, other, chunks)
    )
    lowrank_local = lax.dynamic_index_in_dim(lowrank_up_map, expert_position, 0, keepdims=False)
    gathered = lax.all_gather(
        jnp.concatenate([d_rows, lowrank_local], axis=0), TENSOR, axis=1, tiled=True
    )

    spread_local = sylvester(stride)
    mixed_blocks, _ = mix_blocks(exchange(chunks, SLAB))
    rotated = finish_rotation(exchange(mixed_blocks, SLAB), spread_local, scaling)

    other = lax.ppermute(other, "c", [(0, 1), (1, 0)])
    neighbour = lax.ppermute(rotated, "c", [(0, 1), (1, 0)])
    pair = pair_products(rotated, neighbour, own, other)
    frozen = lax.psum_scatter(pair, "z", scatter_dimension=0, tiled=False)

    d_full = gathered[:slot_rows]
    lowrank_full = gathered[slot_rows:]
    adapter_grad = LOWRANK_SCALE * lax.dot_general(
        d_full, lowrank_full, (((1,), (1,)), ((), ())), preferred_element_type=F32
    )
    adapter_grad = adapter_grad.astype(BF)
    main = dot(d_full, weights, ((1,), (1,)))
    down_map_gradient = dot(rotated, adapter_grad, ((0,), (0,)))
    d_chunks = exchange(
        backward_chunks(main, adapter_grad, lowrank_down_map, rotated, spread_local, scaling), SLAB
    )
    d_mixed, sums = mix_blocks(d_chunks)
    rest = slot_rows - LANES
    row_total = jnp.concatenate([sums[ROWS + 2], sums[ROWS + 1, rest : 2 * rest]])
    d_mixed = exchange(d_mixed, SLAB)
    hidden_gradient = finish_gradient(d_mixed, signs)

    totals = jnp.concatenate(
        [part.astype(BF).reshape(devices, capacity) for part in split(row_total)], axis=1
    )
    totals = jnp.pad(totals, ((0, 0), (0, columns - 2 * capacity)))
    parcel = exchange(build_parcel(frozen, d_mixed, lowrank_local, d_rows, totals), EXPERT)
    mixed, up_map_gradient, gates_gradient = open_parcel(
        parcel, experts.T, gates.T, target, rank
    )
    return (mixed, hidden_gradient, down_map_gradient, up_map_gradient, gates_gradient.T)


def solution(mesh):
    owners, tensor = mesh.devices.shape
    split = Mesh(
        mesh.devices.reshape(EXPERT_COUNT, owners // EXPERT_COUNT, tensor // 2, 2),
        ("e", "r", "z", "c"),
    )
    every = EXPERT + TENSOR
    placed = (
        P(None, every),
        P(every, None),
        P(every, None),
        P(every),
        P(every, None),
        P(None, None, TENSOR),
        P(EXPERT, None),
        P(EXPERT, None),
        P(EXPERT, TENSOR),
    )
    return jax.shard_map(
        body,
        mesh=split,
        in_specs=placed,
        out_specs=(
            P(EXPERT, TENSOR),
            P(None, every),
            P(every, None),
            P(None, None, TENSOR),
            P(EXPERT, None),
        ),
        check_vma=False,
    )
```

```python
import math

import jax
import jax.numpy as jnp
import numpy as np
from jax import lax
from jax.experimental import pallas as pl
from jax.experimental.pallas import tpu as pltpu
from jax.sharding import Mesh
from jax.sharding import PartitionSpec as P

HIDDEN_UNITS = 16384
EXPERT_COUNT = 8
LOWRANK_SCALE = 0.5
HIGH_ACCURACY = lax.Precision.HIGHEST
BF = jnp.bfloat16
F32 = jnp.float32
EXPERT = ("e", "r")
TENSOR = ("z", "c")
SLAB = ("r", "z", "c")
LANES = 128
TILE = 8
ROWS = 5


def sylvester(count):
    table = np.ones((1, 1), np.float32)
    while table.shape[0] < count:
        table = np.kron(np.array([[1.0, 1.0], [1.0, -1.0]], np.float32), table)
    return jnp.asarray(table, BF)


def exchange(value, axes):
    return lax.all_to_all(value, axes, split_axis=0, concat_axis=0, tiled=True)


def dot(left, right, dims=((1,), (0,))):
    return lax.dot_general(left, right, (dims, ((), ())), preferred_element_type=F32)


def placement(blocks, rows):
    out_row = lax.broadcasted_iota(jnp.int32, (blocks * TILE, blocks * rows), 0)
    in_row = lax.broadcasted_iota(jnp.int32, (blocks * TILE, blocks * rows), 1)
    k = out_row % TILE
    return jnp.where((k < rows) & (out_row // TILE * rows + k == in_row), 1.0, 0.0).astype(BF)


def rider_rows(peers, k):
    out_row = lax.broadcasted_iota(jnp.int32, (peers * TILE, peers), 0)
    in_row = lax.broadcasted_iota(jnp.int32, (peers * TILE, peers), 1)
    return jnp.where(out_row == in_row * TILE + k, 1.0, 0.0).astype(BF)


def whole(kernel, out_shape, *operands):
    return pl.pallas_call(
        kernel,
        out_shape=out_shape,
        compiler_params=pltpu.CompilerParams(vmem_limit_bytes=32 * 1024 * 1024),
    )(*operands)


def route(experts, gates, output_gradient, replicas, capacity):
    choices, tokens = experts.shape
    columns = output_gradient.shape[1]
    rows = EXPERT_COUNT * replicas * capacity

    def kernel(experts_ref, gates_ref, grad_ref, out_ref, target_ref):
        ids = experts_ref[...]
        gate = gates_ref[...]
        expert = lax.broadcasted_iota(jnp.int32, (EXPERT_COUNT, tokens), 0)
        named = [
            jnp.where(ids[k : k + 1] == expert, 1.0, 0.0) for k in range(choices)
        ]
        row = lax.broadcasted_iota(jnp.int32, (tokens, tokens), 0)
        col = lax.broadcasted_iota(jnp.int32, (tokens, tokens), 1)
        upper = jnp.where(row < col, 1.0, 0.0).astype(BF)
        earlier = dot(sum(named).astype(BF), upper)
        place = lax.broadcasted_iota(jnp.int32, (rows, tokens), 0).astype(F32)
        block = jnp.floor((place + 0.5) * (1.0 / capacity))
        owner = jnp.floor((place + 0.5) * (1.0 / (replicas * capacity)))
        slot_row = (place + capacity * (owner - block)).astype(jnp.int32)
        picked = jnp.zeros((rows, tokens), F32)
        weight = jnp.zeros((rows, tokens), F32)
        targets = []
        for k in range(choices):
            slot = jnp.sum(earlier * named[k], axis=0, keepdims=True).astype(jnp.int32)
            target = ids[k : k + 1] * capacity + slot
            match = jnp.where(target == slot_row, 1.0, 0.0)
            picked = picked + match
            weight = weight + match * gate[k : k + 1]
            earlier = earlier + named[k]
            targets.append(target)
        values = dot(picked.astype(BF), grad_ref[...])
        out_ref[...] = (values * jnp.sum(weight, axis=1, keepdims=True)).astype(BF)
        choice = lax.broadcasted_iota(jnp.int32, (choices, tokens), 0)
        chosen = jnp.broadcast_to(targets[0], (choices, tokens))
        for k in range(1, choices):
            chosen = jnp.where(choice == k, targets[k], chosen)
        target_ref[...] = chosen

    out = (
        jax.ShapeDtypeStruct((rows, columns), BF),
        jax.ShapeDtypeStruct((choices, tokens), jnp.int32),
    )
    return whole(kernel, out, experts, gates, output_gradient)


def build_parcel(frozen, d_mixed, up_map, d_rows, totals):
    height, columns = frozen.shape
    devices = totals.shape[0]
    rank = up_map.shape[0]
    peers = d_mixed.shape[0]
    rest = height - LANES

    def kernel(frozen_ref, mixed_ref, up_ref, rows_ref, totals_ref, out_ref):
        flat = mixed_ref[...].reshape(peers * TILE, LANES)
        adapter = read_riders(flat, peers, rest).astype(BF)
        replicas = devices // EXPERT_COUNT
        share = rank // replicas
        slots = frozen_ref[...] + (LOWRANK_SCALE / replicas) * dot(
            adapter, up_ref[...], ((0,), (0,))
        )
        row = lax.broadcasted_iota(jnp.int32, (share, rank), 0)
        col = lax.broadcasted_iota(jnp.int32, (share, rank), 1)
        chosen = jnp.where(col == row + lax.axis_index("r") * share, 1.0, 0.0).astype(BF)
        part = dot(chosen, adapter).astype(BF)
        up = (LOWRANK_SCALE * dot(part, rows_ref[...])).astype(BF)
        out_ref[:, :share, :] = jnp.broadcast_to(up[None], (devices, share, columns))
        rows = dot(placement(devices, ROWS), slots.astype(BF))
        rows += dot(rider_rows(devices, ROWS), totals_ref[...])
        rows = rows.reshape(devices, TILE, columns)[:, : ROWS + 1]
        out_ref[:, share:, :] = rows.astype(BF)

    share = rank * EXPERT_COUNT // devices
    out = jax.ShapeDtypeStruct((devices, share + ROWS + 1, columns), BF)
    return whole(kernel, out, frozen, d_mixed, up_map, d_rows, totals)


def open_parcel(parcel, experts, gates, target, rank):
    devices, height, columns = parcel.shape
    choices, tokens = experts.shape
    replicas = devices // EXPERT_COUNT
    share = rank // replicas

    def kernel(parcel_ref, experts_ref, gates_ref, target_ref, mixed_ref, up_ref, grad_ref):
        values = parcel_ref[...].astype(F32)
        up_ref[...] = values[:, :share].reshape(EXPERT_COUNT, rank, columns)
        rest = values[:, share:].reshape(EXPERT_COUNT, replicas, ROWS + 1, columns).sum(axis=1)
        gate = gates_ref[...]
        target = target_ref[...]
        slot = target - experts_ref[...] * ROWS
        c = lax.broadcasted_iota(jnp.int32, (ROWS + 1, tokens), 0)
        mixed = jnp.zeros((tokens, columns), F32)
        for e in range(EXPERT_COUNT):
            mixer = jnp.zeros((ROWS + 1, tokens), F32)
            for k in range(choices):
                hit = (target[k : k + 1] == e * ROWS + c) & (c < ROWS)
                mixer = mixer + jnp.where(hit, gate[k : k + 1], 0.0)
            mixed = mixed + lax.dot_general(
                mixer,
                rest[e],
                (((0,), (0,)), ((), ())),
                precision=HIGH_ACCURACY,
                preferred_element_type=F32,
            )
        mixed_ref[...] = mixed.astype(BF)
        totals = jnp.concatenate(
            [rest[e, ROWS : ROWS + 1, :LANES] for e in range(EXPERT_COUNT)], axis=0
        )
        totals = (totals * (1.0 / replicas)).astype(BF)
        expert = lax.broadcasted_iota(jnp.int32, (EXPERT_COUNT, tokens), 0)
        lane = lax.broadcasted_iota(jnp.int32, (LANES, tokens), 0)
        grads = []
        for k in range(choices):
            named = jnp.where(experts_ref[k : k + 1, :] == expert, 1.0, 0.0).astype(BF)
            by_lane = dot(totals, named, ((0,), (0,)))
            at = slot[k : k + 1]
            hit = (lane == at) | (lane == at + ROWS)
            grads.append(jnp.sum(jnp.where(hit, by_lane, 0.0), axis=0, keepdims=True))
        grad_ref[...] = jnp.concatenate(grads, axis=0) / gate

    out = (
        jax.ShapeDtypeStruct((tokens, columns), BF),
        jax.ShapeDtypeStruct((EXPERT_COUNT, rank, columns), F32),
        jax.ShapeDtypeStruct((choices, tokens), F32),
    )
    return whole(kernel, out, parcel, experts, gates, target)


def dequantize(codes, scales, depth, columns):
    stride, width = codes.shape
    groups = scales.shape[0]
    size = stride // groups

    def kernel(codes_ref, scales_ref, all_ref, own_ref, other_ref):
        first = lax.axis_index("c") == 0
        for group in range(groups):
            rows = slice(group * size, (group + 1) * size)
            values = codes_ref[rows, :].astype(F32) * scales_ref[group : group + 1, :]
            all_ref[rows, :] = values.astype(BF)
            low, high = values[:, :columns], values[:, columns:]
            own_ref[0, rows, :] = jnp.where(first, low, high).astype(BF)
            other_ref[0, rows, :] = jnp.where(first, high, low).astype(BF)

    half = pl.BlockSpec((1, stride, columns), lambda z: (z, 0, 0))
    halves = jax.ShapeDtypeStruct((depth, stride, columns), BF)
    return pl.pallas_call(
        kernel,
        grid=(depth,),
        in_specs=[
            pl.BlockSpec((stride, 2 * columns), lambda z: (0, z)),
            pl.BlockSpec((groups, 2 * columns), lambda z: (0, z)),
        ],
        out_specs=(pl.BlockSpec((stride, 2 * columns), lambda z: (0, z)), half, half),
        out_shape=(jax.ShapeDtypeStruct((stride, width), BF), halves, halves),
        cost_estimate=pl.CostEstimate(
            flops=2 * stride * width, bytes_accessed=6 * stride * width, transcendentals=0
        ),
        compiler_params=pltpu.CompilerParams(vmem_limit_bytes=32 * 1024 * 1024),
    )(codes, scales)


def pair_products(rotated, neighbour, own, other):
    depth, stride, columns = own.shape
    height = rotated.shape[0]
    step = 2

    def kernel(rotated_ref, neighbour_ref, own_ref, other_ref, out_ref):
        for z in range(step):
            total = dot(rotated_ref[...], own_ref[z]) + dot(neighbour_ref[...], other_ref[z])
            out_ref[z] = total

    rows = pl.BlockSpec((height, stride), lambda z: (0, 0))
    half = pl.BlockSpec((step, stride, columns), lambda z: (z, 0, 0))
    return pl.pallas_call(
        kernel,
        grid=(depth // step,),
        in_specs=[rows, rows, half, half],
        out_specs=pl.BlockSpec((step, height, columns), lambda z: (z, 0, 0)),
        out_shape=jax.ShapeDtypeStruct((depth, height, columns), F32),
        cost_estimate=pl.CostEstimate(
            flops=4 * height * stride * depth * columns,
            bytes_accessed=4 * depth * columns * (stride + height),
            transcendentals=0,
        ),
        compiler_params=pltpu.CompilerParams(vmem_limit_bytes=32 * 1024 * 1024),
    )(rotated, neighbour, own, other)


def rank_riders(columns, peers):
    rest = columns.shape[1] - LANES
    pad = jnp.zeros((peers, LANES - rest), BF)
    tail = jnp.concatenate([columns[:, LANES:], pad], axis=1)
    riders = dot(rider_rows(peers, ROWS), columns[:, :LANES])
    return riders + dot(rider_rows(peers, ROWS + 1), tail)


def read_riders(flat, peers, rest):
    first = dot(rider_rows(peers, ROWS), flat, ((0,), (0,)))
    second = dot(rider_rows(peers, ROWS + 1), flat, ((0,), (0,)))
    return jnp.concatenate([first, second[:, :rest]], axis=1)


def to_chunks(values, signs, d_rows, up_map):
    height, stride = values.shape
    halves = stride // LANES
    blocks = height // ROWS
    peers = halves * blocks

    def kernel(values_ref, signs_ref, rows_ref, up_ref, out_ref):
        sign = (2 * signs_ref[...] - 1).astype(F32)
        signed = (values_ref[...].astype(F32) * sign).astype(BF)
        riders = rank_riders(dot(up_ref[...], rows_ref[...], ((1,), (1,))).astype(BF), peers)
        place = placement(blocks, ROWS)
        for half in range(halves):
            part = dot(place, signed[:, half * LANES : (half + 1) * LANES])
            part += riders[half * blocks * TILE : (half + 1) * blocks * TILE]
            part = part.astype(BF).reshape(blocks, TILE, LANES)
            out_ref[half * blocks : (half + 1) * blocks] = part

    out = jax.ShapeDtypeStruct((peers, TILE, LANES), BF)
    return whole(kernel, out, values, signs.reshape(1, stride), d_rows, up_map)


def hadamard(parts):
    step = 1
    while step < len(parts):
        for low in range(len(parts)):
            if low & step == 0:
                one, two = parts[low], parts[low + step]
                parts[low], parts[low + step] = one + two, one - two
        step *= 2
    return parts


def mix_blocks(chunks):
    def kernel(chunks_ref, out_ref, sum_ref):
        values = chunks_ref[...].astype(F32)
        mixed = hadamard([values[p] for p in range(values.shape[0])])
        row = lax.broadcasted_iota(jnp.int32, (TILE, LANES), 0)
        sum_ref[...] = mixed[0]
        for p, part in enumerate(mixed):
            out_ref[p] = jnp.where(row < ROWS, part, mixed[0]).astype(BF)

    out = jax.ShapeDtypeStruct(chunks.shape, BF), jax.ShapeDtypeStruct((TILE, LANES), F32)
    return whole(kernel, out, chunks)


def gather_rows(chunks, blocks):
    flat = chunks.reshape(-1, LANES)
    place = placement(blocks, ROWS)
    size = blocks * TILE
    halves = flat.shape[0] // size
    parts = [
        dot(place, flat[half * size : (half + 1) * size], ((0,), (0,))) for half in range(halves)
    ]
    return jnp.concatenate(parts, axis=1)


def finish_rotation(chunks, spread, scaling, replicas):
    peers = chunks.shape[0]
    blocks = peers * LANES // spread.shape[0]
    rest = blocks * ROWS - LANES

    def kernel(chunks_ref, spread_ref, out_ref, grad_ref):
        chunk_values = chunks_ref[...]
        values = gather_rows(chunk_values, blocks).astype(BF)
        out_ref[...] = (dot(values, spread_ref[...]) * scaling).astype(BF)
        grad = read_riders(chunk_values.reshape(peers * TILE, LANES), peers, rest)
        grad_ref[...] = (grad * (LOWRANK_SCALE / replicas)).astype(BF)

    out = (
        jax.ShapeDtypeStruct((blocks * ROWS, spread.shape[0]), BF),
        jax.ShapeDtypeStruct((peers, blocks * ROWS), BF),
    )
    return whole(kernel, out, chunks, spread)


def finish_gradient(chunks, signs):
    stride = signs.shape[0]
    blocks = chunks.shape[0] * LANES // stride

    def kernel(chunks_ref, signs_ref, out_ref):
        sign = (2 * signs_ref[...] - 1).astype(F32)
        out_ref[...] = (gather_rows(chunks_ref[...], blocks) * sign).astype(BF)

    out = jax.ShapeDtypeStruct((blocks * ROWS, stride), BF)
    return whole(kernel, out, chunks, signs.reshape(1, stride))


def backward_chunks(main, adapter_grad, down_map, rotated, spread, scaling):
    height, stride = main.shape
    halves = stride // LANES
    blocks = height // ROWS
    peers = halves * blocks
    rest = height - LANES

    def kernel(main_ref, grad_ref, down_ref, rotated_ref, spread_ref, out_ref):
        rotated_value = rotated_ref[...]
        down = down_ref[...]
        d_rotated = main_ref[...] + dot(grad_ref[...], down, ((0,), (1,)))
        local = dot(d_rotated.astype(BF), spread_ref[...])
        local = (local * scaling).astype(BF)
        product = rotated_value.astype(F32) * d_rotated
        totals = lax.dot_general(
            jnp.ones((TILE, stride), F32),
            product,
            (((1,), (1,)), ((), ())),
            precision=HIGH_ACCURACY,
            preferred_element_type=F32,
        )
        adapter = dot(down, rotated_value, ((0,), (1,))).astype(BF)
        riders = rank_riders(adapter, peers)
        row_tail = jnp.concatenate(
            [totals[:, LANES:], jnp.zeros((TILE, LANES - rest), F32)], axis=1
        )
        row_tail = pltpu.roll(row_tail, rest, 1)
        k = lax.broadcasted_iota(jnp.int32, (TILE, LANES), 0)
        extra = jnp.where(k == ROWS + 2, totals[:, :LANES], 0.0)
        extra += jnp.where(k == ROWS + 1, row_tail, 0.0)
        place = placement(blocks, ROWS)
        for half in range(halves):
            part = dot(place, local[:, half * LANES : (half + 1) * LANES])
            part += riders[half * blocks * TILE : (half + 1) * blocks * TILE]
            part = part.reshape(blocks, TILE, LANES) + extra[None]
            out_ref[half * blocks : (half + 1) * blocks] = part.astype(BF)

    out = jax.ShapeDtypeStruct((peers, TILE, LANES), BF)
    return whole(kernel, out, main, adapter_grad, down_map, rotated, spread)


def split(values):
    high = lax.reduce_precision(values, 8, 7)
    return high, lax.reduce_precision(values - high, 8, 7)


def body(
    hidden, codes, scales, signs, lowrank_down_map, lowrank_up_map, experts, gates, output_gradient
):
    slot_rows, stride = hidden.shape
    replicas, depth = lax.axis_size("r"), lax.axis_size("z")
    devices = EXPERT_COUNT * replicas
    rank = lowrank_down_map.shape[1]
    expert_position = lax.axis_index("e")
    capacity = slot_rows // devices
    columns = output_gradient.shape[1]
    scaling = 1.0 / math.sqrt(HIDDEN_UNITS)

    outgoing, target = route(experts.T, gates.T, output_gradient, replicas, capacity)
    weights, own, other = dequantize(codes, scales, depth, columns)
    d_rows = exchange(outgoing, EXPERT)
    arrived = lax.ppermute(other, "c", [(0, 1), (1, 0)])
    d_rows, weights, own, _ = lax.optimization_barrier((d_rows, weights, own, other))
    lowrank_local = lax.dynamic_index_in_dim(lowrank_up_map, expert_position, 0, keepdims=False)
    d_full = lax.all_gather(d_rows, TENSOR, axis=1, tiled=True)

    spread_local = sylvester(stride)
    chunks = to_chunks(hidden, signs, d_rows, lowrank_local)
    mixed_blocks, _ = mix_blocks(exchange(chunks, SLAB))
    rotated, adapter_grad = finish_rotation(
        exchange(mixed_blocks, SLAB), spread_local, scaling, replicas
    )

    neighbour = lax.ppermute(rotated, "c", [(0, 1), (1, 0)])
    pair = pair_products(rotated, neighbour, own, arrived)
    frozen = lax.psum_scatter(pair, "z", scatter_dimension=0, tiled=False)

    main = dot(d_full, weights, ((1,), (1,)))
    down_map_gradient = dot(rotated, adapter_grad, ((0,), (1,)))
    d_chunks = exchange(
        backward_chunks(main, adapter_grad, lowrank_down_map, rotated, spread_local, scaling), SLAB
    )
    d_mixed, sums = mix_blocks(d_chunks)
    rest = slot_rows - LANES
    row_total = jnp.concatenate([sums[ROWS + 2], sums[ROWS + 1, rest : 2 * rest]])
    d_mixed = exchange(d_mixed, SLAB)
    hidden_gradient = finish_gradient(d_mixed, signs)

    totals = jnp.concatenate(
        [part.astype(BF).reshape(devices, capacity) for part in split(row_total)], axis=1
    )
    totals = jnp.pad(totals, ((0, 0), (0, columns - 2 * capacity)))
    parcel = exchange(build_parcel(frozen, d_mixed, lowrank_local, d_rows, totals), EXPERT)
    mixed, up_map_gradient, gates_gradient = open_parcel(
        parcel, experts.T, gates.T, target, rank
    )
    return (mixed, hidden_gradient, down_map_gradient, up_map_gradient, gates_gradient.T)


def solution(mesh):
    owners, tensor = mesh.devices.shape
    split = Mesh(
        mesh.devices.reshape(EXPERT_COUNT, owners // EXPERT_COUNT, tensor // 2, 2),
        ("e", "r", "z", "c"),
    )
    every = EXPERT + TENSOR
    placed = (
        P(None, every),
        P(every, None),
        P(every, None),
        P(every),
        P(every, None),
        P(None, None, TENSOR),
        P(EXPERT, None),
        P(EXPERT, None),
        P(EXPERT, TENSOR),
    )
    return jax.shard_map(
        body,
        mesh=split,
        in_specs=placed,
        out_specs=(
            P(EXPERT, TENSOR),
            P(None, every),
            P(every, None),
            P(None, None, TENSOR),
            P(EXPERT, None),
        ),
        check_vma=False,
    )
```

```python
import math

import jax
import jax.numpy as jnp
import numpy as np
from jax import lax
from jax.experimental import pallas as pl
from jax.experimental.pallas import tpu as pltpu
from jax.sharding import Mesh
from jax.sharding import PartitionSpec as P

HIDDEN_UNITS = 16384
EXPERT_COUNT = 8
LOWRANK_SCALE = 0.5
HIGH_ACCURACY = lax.Precision.HIGHEST
BF = jnp.bfloat16
F32 = jnp.float32
EXPERT = ("e", "r")
TENSOR = ("z", "c")
SLAB = ("r", "z", "c")
LANES = 128
TILE = 8
ROWS = 5


def sylvester(count):
    table = np.ones((1, 1), np.float32)
    while table.shape[0] < count:
        table = np.kron(np.array([[1.0, 1.0], [1.0, -1.0]], np.float32), table)
    return jnp.asarray(table, BF)


def exchange(value, axes):
    return lax.all_to_all(value, axes, split_axis=0, concat_axis=0, tiled=True)


def dot(left, right, dims=((1,), (0,))):
    return lax.dot_general(left, right, (dims, ((), ())), preferred_element_type=F32)


def placement(blocks, rows):
    out_row = lax.broadcasted_iota(jnp.int32, (blocks * TILE, blocks * rows), 0)
    in_row = lax.broadcasted_iota(jnp.int32, (blocks * TILE, blocks * rows), 1)
    k = out_row % TILE
    return jnp.where((k < rows) & (out_row // TILE * rows + k == in_row), 1.0, 0.0).astype(BF)


def rider_rows(peers, k):
    out_row = lax.broadcasted_iota(jnp.int32, (peers * TILE, peers), 0)
    in_row = lax.broadcasted_iota(jnp.int32, (peers * TILE, peers), 1)
    return jnp.where(out_row == in_row * TILE + k, 1.0, 0.0).astype(BF)


def whole(kernel, out_shape, *operands):
    return pl.pallas_call(
        kernel,
        out_shape=out_shape,
        compiler_params=pltpu.CompilerParams(vmem_limit_bytes=32 * 1024 * 1024),
    )(*operands)


def route(experts, gates, output_gradient, replicas, capacity):
    choices, tokens = experts.shape
    columns = output_gradient.shape[1]
    rows = EXPERT_COUNT * replicas * capacity

    def kernel(experts_ref, gates_ref, grad_ref, out_ref, target_ref):
        ids = experts_ref[...]
        gate = gates_ref[...]
        expert = lax.broadcasted_iota(jnp.int32, (EXPERT_COUNT, tokens), 0)
        named = [
            jnp.where(ids[k : k + 1] == expert, 1.0, 0.0) for k in range(choices)
        ]
        row = lax.broadcasted_iota(jnp.int32, (tokens, tokens), 0)
        col = lax.broadcasted_iota(jnp.int32, (tokens, tokens), 1)
        upper = jnp.where(row < col, 1.0, 0.0).astype(BF)
        earlier = dot(sum(named).astype(BF), upper)
        place = lax.broadcasted_iota(jnp.int32, (rows, tokens), 0).astype(F32)
        block = jnp.floor((place + 0.5) * (1.0 / capacity))
        owner = jnp.floor((place + 0.5) * (1.0 / (replicas * capacity)))
        slot_row = (place + capacity * (owner - block)).astype(jnp.int32)
        picked = jnp.zeros((rows, tokens), F32)
        weight = jnp.zeros((rows, tokens), F32)
        targets = []
        for k in range(choices):
            slot = jnp.sum(earlier * named[k], axis=0, keepdims=True).astype(jnp.int32)
            target = ids[k : k + 1] * capacity + slot
            match = jnp.where(target == slot_row, 1.0, 0.0)
            picked = picked + match
            weight = weight + match * gate[k : k + 1]
            earlier = earlier + named[k]
            targets.append(target)
        values = dot(picked.astype(BF), grad_ref[...])
        out_ref[...] = (values * jnp.sum(weight, axis=1, keepdims=True)).astype(BF)
        choice = lax.broadcasted_iota(jnp.int32, (choices, tokens), 0)
        chosen = jnp.broadcast_to(targets[0], (choices, tokens))
        for k in range(1, choices):
            chosen = jnp.where(choice == k, targets[k], chosen)
        target_ref[...] = chosen

    out = (
        jax.ShapeDtypeStruct((rows, columns), BF),
        jax.ShapeDtypeStruct((choices, tokens), jnp.int32),
    )
    return pl.pallas_call(kernel, out_shape=out)(experts, gates, output_gradient)


def build_parcel(frozen, d_mixed, up_map, d_rows, totals):
    height, columns = frozen.shape
    devices = totals.shape[0]
    rank = up_map.shape[0]
    peers = d_mixed.shape[0]
    rest = height - LANES

    def kernel(frozen_ref, mixed_ref, up_ref, rows_ref, totals_ref, out_ref):
        flat = mixed_ref[...].reshape(peers * TILE, LANES)
        first = dot(rider_rows(peers, ROWS), flat, ((0,), (0,)))
        second = dot(rider_rows(peers, ROWS + 1), flat, ((0,), (0,)))
        adapter = jnp.concatenate([first, second[:, :rest]], axis=1).astype(BF)
        replicas = devices // EXPERT_COUNT
        share = rank // replicas
        slots = frozen_ref[...] + (LOWRANK_SCALE / replicas) * dot(
            adapter, up_ref[...], ((0,), (0,))
        )
        row = lax.broadcasted_iota(jnp.int32, (share, rank), 0)
        col = lax.broadcasted_iota(jnp.int32, (share, rank), 1)
        chosen = jnp.where(col == row + lax.axis_index("r") * share, 1.0, 0.0).astype(BF)
        part = dot(chosen, adapter).astype(BF)
        up = (LOWRANK_SCALE * dot(part, rows_ref[...])).astype(BF)
        out_ref[:, :share, :] = jnp.broadcast_to(up[None], (devices, share, columns))
        rows = dot(placement(devices, ROWS), slots.astype(BF))
        rows += dot(rider_rows(devices, ROWS), totals_ref[...])
        rows = rows.reshape(devices, TILE, columns)[:, : ROWS + 1]
        out_ref[:, share:, :] = rows.astype(BF)

    share = rank * EXPERT_COUNT // devices
    out = jax.ShapeDtypeStruct((devices, share + ROWS + 1, columns), BF)
    return whole(kernel, out, frozen, d_mixed, up_map, d_rows, totals)


def open_parcel(parcel, experts, gates, target, rank):
    devices, height, columns = parcel.shape
    choices, tokens = experts.shape
    replicas = devices // EXPERT_COUNT
    share = rank // replicas

    def kernel(parcel_ref, experts_ref, gates_ref, target_ref, mixed_ref, up_ref, grad_ref):
        values = parcel_ref[...].astype(F32)
        up_ref[...] = values[:, :share].reshape(EXPERT_COUNT, rank, columns)
        rest = values[:, share:].reshape(EXPERT_COUNT, replicas, ROWS + 1, columns).sum(axis=1)
        gate = gates_ref[...]
        target = target_ref[...]
        slot = target - experts_ref[...] * ROWS
        c = lax.broadcasted_iota(jnp.int32, (ROWS + 1, tokens), 0)
        mixed = jnp.zeros((tokens, columns), F32)
        for e in range(EXPERT_COUNT):
            mixer = jnp.zeros((ROWS + 1, tokens), F32)
            for k in range(choices):
                hit = (target[k : k + 1] == e * ROWS + c) & (c < ROWS)
                mixer = mixer + jnp.where(hit, gate[k : k + 1], 0.0)
            mixed = mixed + lax.dot_general(
                mixer,
                rest[e],
                (((0,), (0,)), ((), ())),
                precision=HIGH_ACCURACY,
                preferred_element_type=F32,
            )
        mixed_ref[...] = mixed.astype(BF)
        totals = jnp.concatenate(
            [rest[e, ROWS : ROWS + 1, :LANES] for e in range(EXPERT_COUNT)], axis=0
        )
        totals = (totals * (1.0 / replicas)).astype(BF)
        expert = lax.broadcasted_iota(jnp.int32, (EXPERT_COUNT, tokens), 0)
        lane = lax.broadcasted_iota(jnp.int32, (LANES, tokens), 0)
        grads = []
        for k in range(choices):
            named = jnp.where(experts_ref[k : k + 1, :] == expert, 1.0, 0.0).astype(BF)
            by_lane = dot(totals, named, ((0,), (0,)))
            at = slot[k : k + 1]
            hit = (lane == at) | (lane == at + ROWS)
            grads.append(jnp.sum(jnp.where(hit, by_lane, 0.0), axis=0, keepdims=True))
        grad_ref[...] = jnp.concatenate(grads, axis=0) / gate

    out = (
        jax.ShapeDtypeStruct((tokens, columns), BF),
        jax.ShapeDtypeStruct((EXPERT_COUNT, rank, columns), F32),
        jax.ShapeDtypeStruct((choices, tokens), F32),
    )
    return whole(kernel, out, parcel, experts, gates, target)


def dequantize(codes, scales, depth, columns):
    stride, width = codes.shape
    groups = scales.shape[0]
    size = stride // groups

    def kernel(codes_ref, scales_ref, all_ref, own_ref, other_ref):
        first = lax.axis_index("c") == 0
        for group in range(groups):
            rows = slice(group * size, (group + 1) * size)
            values = codes_ref[rows, :].astype(F32) * scales_ref[group : group + 1, :]
            all_ref[rows, :] = values.astype(BF)
            low, high = values[:, :columns], values[:, columns:]
            own_ref[0, rows, :] = jnp.where(first, low, high).astype(BF)
            other_ref[0, rows, :] = jnp.where(first, high, low).astype(BF)

    half = pl.BlockSpec((1, stride, columns), lambda z: (z, 0, 0))
    halves = jax.ShapeDtypeStruct((depth, stride, columns), BF)
    return pl.pallas_call(
        kernel,
        grid=(depth,),
        in_specs=[
            pl.BlockSpec((stride, 2 * columns), lambda z: (0, z)),
            pl.BlockSpec((groups, 2 * columns), lambda z: (0, z)),
        ],
        out_specs=(pl.BlockSpec((stride, 2 * columns), lambda z: (0, z)), half, half),
        out_shape=(jax.ShapeDtypeStruct((stride, width), BF), halves, halves),
        cost_estimate=pl.CostEstimate(
            flops=2 * stride * width, bytes_accessed=6 * stride * width, transcendentals=0
        ),
        compiler_params=pltpu.CompilerParams(vmem_limit_bytes=32 * 1024 * 1024),
    )(codes, scales)


def pair_products(rotated, neighbour, own, other):
    depth, stride, columns = own.shape
    height = rotated.shape[0]
    step = 2

    def kernel(rotated_ref, neighbour_ref, own_ref, other_ref, out_ref):
        for z in range(step):
            total = dot(rotated_ref[...], own_ref[z]) + dot(neighbour_ref[...], other_ref[z])
            out_ref[z] = total

    rows = pl.BlockSpec((height, stride), lambda z: (0, 0))
    half = pl.BlockSpec((step, stride, columns), lambda z: (z, 0, 0))
    return pl.pallas_call(
        kernel,
        grid=(depth // step,),
        in_specs=[rows, rows, half, half],
        out_specs=pl.BlockSpec((step, height, columns), lambda z: (z, 0, 0)),
        out_shape=jax.ShapeDtypeStruct((depth, height, columns), F32),
        cost_estimate=pl.CostEstimate(
            flops=4 * height * stride * depth * columns,
            bytes_accessed=4 * depth * columns * (stride + height),
            transcendentals=0,
        ),
        compiler_params=pltpu.CompilerParams(vmem_limit_bytes=32 * 1024 * 1024),
    )(rotated, neighbour, own, other)


def to_chunks(values, signs):
    height, stride = values.shape
    halves = stride // LANES
    blocks = height // ROWS

    def kernel(values_ref, signs_ref, out_ref):
        sign = (2 * signs_ref[...] - 1).astype(F32)
        signed = (values_ref[...].astype(F32) * sign).astype(BF)
        place = placement(blocks, ROWS)
        for half in range(halves):
            part = dot(place, signed[:, half * LANES : (half + 1) * LANES])
            part = part.astype(BF).reshape(blocks, TILE, LANES)
            out_ref[half * blocks : (half + 1) * blocks] = part

    out = jax.ShapeDtypeStruct((halves * blocks, TILE, LANES), BF)
    return whole(kernel, out, values, signs.reshape(1, stride))


def hadamard(parts):
    step = 1
    while step < len(parts):
        for low in range(len(parts)):
            if low & step == 0:
                one, two = parts[low], parts[low + step]
                parts[low], parts[low + step] = one + two, one - two
        step *= 2
    return parts


def mix_blocks(chunks):
    def kernel(chunks_ref, out_ref, sum_ref):
        values = chunks_ref[...].astype(F32)
        mixed = hadamard([values[p] for p in range(values.shape[0])])
        row = lax.broadcasted_iota(jnp.int32, (TILE, LANES), 0)
        sum_ref[...] = mixed[0]
        for p, part in enumerate(mixed):
            out_ref[p] = jnp.where(row < ROWS, part, mixed[0]).astype(BF)

    out = jax.ShapeDtypeStruct(chunks.shape, BF), jax.ShapeDtypeStruct((TILE, LANES), F32)
    return whole(kernel, out, chunks)


def gather_rows(chunks, blocks):
    flat = chunks.reshape(-1, LANES)
    place = placement(blocks, ROWS)
    size = blocks * TILE
    halves = flat.shape[0] // size
    parts = [
        dot(place, flat[half * size : (half + 1) * size], ((0,), (0,))) for half in range(halves)
    ]
    return jnp.concatenate(parts, axis=1)


def finish_rotation(chunks, spread, scaling):
    blocks = chunks.shape[0] * LANES // spread.shape[0]

    def kernel(chunks_ref, spread_ref, out_ref):
        values = gather_rows(chunks_ref[...], blocks).astype(BF)
        out_ref[...] = (dot(values, spread_ref[...]) * scaling).astype(BF)

    out = jax.ShapeDtypeStruct((blocks * ROWS, spread.shape[0]), BF)
    return whole(kernel, out, chunks, spread)


def finish_gradient(chunks, signs):
    stride = signs.shape[0]
    blocks = chunks.shape[0] * LANES // stride

    def kernel(chunks_ref, signs_ref, out_ref):
        sign = (2 * signs_ref[...] - 1).astype(F32)
        out_ref[...] = (gather_rows(chunks_ref[...], blocks) * sign).astype(BF)

    out = jax.ShapeDtypeStruct((blocks * ROWS, stride), BF)
    return whole(kernel, out, chunks, signs.reshape(1, stride))


def backward_chunks(main, adapter_grad, down_map, rotated, spread, scaling):
    height, stride = main.shape
    halves = stride // LANES
    blocks = height // ROWS
    peers = halves * blocks
    rest = height - LANES

    def kernel(main_ref, grad_ref, down_ref, rotated_ref, spread_ref, out_ref):
        rotated_value = rotated_ref[...]
        down = down_ref[...]
        d_rotated = main_ref[...] + dot(grad_ref[...], down, ((1,), (1,)))
        local = dot(d_rotated.astype(BF), spread_ref[...])
        local = (local * scaling).astype(BF)
        product = rotated_value.astype(F32) * d_rotated
        totals = lax.dot_general(
            jnp.ones((TILE, stride), F32),
            product,
            (((1,), (1,)), ((), ())),
            precision=HIGH_ACCURACY,
            preferred_element_type=F32,
        )
        adapter = dot(down, rotated_value, ((0,), (1,))).astype(BF)
        pad = jnp.zeros((peers, LANES - rest), BF)
        riders = dot(rider_rows(peers, ROWS), adapter[:, :LANES])
        tail = jnp.concatenate([adapter[:, LANES:], pad], axis=1)
        riders += dot(rider_rows(peers, ROWS + 1), tail)
        row_tail = jnp.concatenate(
            [totals[:, LANES:], jnp.zeros((TILE, LANES - rest), F32)], axis=1
        )
        row_tail = pltpu.roll(row_tail, rest, 1)
        k = lax.broadcasted_iota(jnp.int32, (TILE, LANES), 0)
        extra = jnp.where(k == ROWS + 2, totals[:, :LANES], 0.0)
        extra += jnp.where(k == ROWS + 1, row_tail, 0.0)
        place = placement(blocks, ROWS)
        for half in range(halves):
            part = dot(place, local[:, half * LANES : (half + 1) * LANES])
            part += riders[half * blocks * TILE : (half + 1) * blocks * TILE]
            part = part.reshape(blocks, TILE, LANES) + extra[None]
            out_ref[half * blocks : (half + 1) * blocks] = part.astype(BF)

    out = jax.ShapeDtypeStruct((peers, TILE, LANES), BF)
    return whole(kernel, out, main, adapter_grad, down_map, rotated, spread)


def split(values):
    high = lax.reduce_precision(values, 8, 7)
    return high, lax.reduce_precision(values - high, 8, 7)


def body(
    hidden, codes, scales, signs, lowrank_down_map, lowrank_up_map, experts, gates, output_gradient
):
    slot_rows, stride = hidden.shape
    replicas, depth = lax.axis_size("r"), lax.axis_size("z")
    devices = EXPERT_COUNT * replicas
    rank = lowrank_down_map.shape[1]
    expert_position = lax.axis_index("e")
    capacity = slot_rows // devices
    columns = output_gradient.shape[1]
    scaling = 1.0 / math.sqrt(HIDDEN_UNITS)

    outgoing, target = route(experts.T, gates.T, output_gradient, replicas, capacity)
    weights, own, other = dequantize(codes, scales, depth, columns)
    d_rows = exchange(outgoing, EXPERT)
    chunks = to_chunks(hidden, signs)
    arrived = lax.ppermute(other, "c", [(0, 1), (1, 0)])
    d_rows, weights, own, arrived, chunks = lax.optimization_barrier(
        (d_rows, weights, own, arrived, chunks)
    )
    lowrank_local = lax.dynamic_index_in_dim(lowrank_up_map, expert_position, 0, keepdims=False)
    gathered = lax.all_gather(
        jnp.concatenate([d_rows, lowrank_local], axis=0), TENSOR, axis=1, tiled=True
    )

    spread_local = sylvester(stride)
    mixed_blocks, _ = mix_blocks(exchange(chunks, SLAB))
    rotated = finish_rotation(exchange(mixed_blocks, SLAB), spread_local, scaling)

    neighbour = lax.ppermute(rotated, "c", [(0, 1), (1, 0)])
    pair = pair_products(rotated, neighbour, own, arrived)
    frozen = lax.psum_scatter(pair, "z", scatter_dimension=0, tiled=False)

    d_full = gathered[:slot_rows]
    lowrank_full = gathered[slot_rows:]
    adapter_grad = LOWRANK_SCALE * lax.dot_general(
        d_full, lowrank_full, (((1,), (1,)), ((), ())), preferred_element_type=F32
    )
    adapter_grad = adapter_grad.astype(BF)
    main = dot(d_full, weights, ((1,), (1,)))
    down_map_gradient = dot(rotated, adapter_grad, ((0,), (0,)))
    d_chunks = exchange(
        backward_chunks(main, adapter_grad, lowrank_down_map, rotated, spread_local, scaling), SLAB
    )
    d_mixed, sums = mix_blocks(d_chunks)
    rest = slot_rows - LANES
    row_total = jnp.concatenate([sums[ROWS + 2], sums[ROWS + 1, rest : 2 * rest]])
    d_mixed = exchange(d_mixed, SLAB)
    hidden_gradient = finish_gradient(d_mixed, signs)

    totals = jnp.concatenate(
        [part.astype(BF).reshape(devices, capacity) for part in split(row_total)], axis=1
    )
    totals = jnp.pad(totals, ((0, 0), (0, columns - 2 * capacity)))
    parcel = exchange(build_parcel(frozen, d_mixed, lowrank_local, d_rows, totals), EXPERT)
    mixed, up_map_gradient, gates_gradient = open_parcel(
        parcel, experts.T, gates.T, target, rank
    )
    return (mixed, hidden_gradient, down_map_gradient, up_map_gradient, gates_gradient.T)


def solution(mesh):
    owners, tensor = mesh.devices.shape
    split = Mesh(
        mesh.devices.reshape(EXPERT_COUNT, owners // EXPERT_COUNT, tensor // 2, 2),
        ("e", "r", "z", "c"),
    )
    every = EXPERT + TENSOR
    placed = (
        P(None, every),
        P(every, None),
        P(every, None),
        P(every),
        P(every, None),
        P(None, None, TENSOR),
        P(EXPERT, None),
        P(EXPERT, None),
        P(EXPERT, TENSOR),
    )
    return jax.shard_map(
        body,
        mesh=split,
        in_specs=placed,
        out_specs=(
            P(EXPERT, TENSOR),
            P(None, every),
            P(every, None),
            P(None, None, TENSOR),
            P(EXPERT, None),
        ),
        check_vma=False,
    )
```

```python
import math

import jax
import jax.numpy as jnp
import numpy as np
from jax import lax
from jax.experimental import pallas as pl
from jax.experimental.pallas import tpu as pltpu
from jax.sharding import Mesh
from jax.sharding import PartitionSpec as P

HIDDEN_UNITS = 16384
EXPERT_COUNT = 8
LOWRANK_SCALE = 0.5
HIGH_ACCURACY = lax.Precision.HIGHEST
BF = jnp.bfloat16
F32 = jnp.float32
EXPERT = ("e", "r")
TENSOR = ("z", "c")
SLAB = ("r", "z", "c")
LANES = 128
TILE = 8
ROWS = 5


def sylvester(count):
    table = np.ones((1, 1), np.float32)
    while table.shape[0] < count:
        table = np.kron(np.array([[1.0, 1.0], [1.0, -1.0]], np.float32), table)
    return jnp.asarray(table, BF)


def exchange(value, axes):
    return lax.all_to_all(value, axes, split_axis=0, concat_axis=0, tiled=True)


def dot(left, right, dims=((1,), (0,))):
    return lax.dot_general(left, right, (dims, ((), ())), preferred_element_type=F32)


def placement(blocks, rows):
    out_row = lax.broadcasted_iota(jnp.int32, (blocks * TILE, blocks * rows), 0)
    in_row = lax.broadcasted_iota(jnp.int32, (blocks * TILE, blocks * rows), 1)
    k = out_row % TILE
    return jnp.where((k < rows) & (out_row // TILE * rows + k == in_row), 1.0, 0.0).astype(BF)


def rider_rows(peers, k):
    out_row = lax.broadcasted_iota(jnp.int32, (peers * TILE, peers), 0)
    in_row = lax.broadcasted_iota(jnp.int32, (peers * TILE, peers), 1)
    return jnp.where(out_row == in_row * TILE + k, 1.0, 0.0).astype(BF)


def whole(kernel, out_shape, *operands):
    return pl.pallas_call(
        kernel,
        out_shape=out_shape,
        compiler_params=pltpu.CompilerParams(vmem_limit_bytes=32 * 1024 * 1024),
    )(*operands)


def route(experts, gates, output_gradient, replicas, capacity):
    choices, tokens = experts.shape
    columns = output_gradient.shape[1]
    rows = EXPERT_COUNT * replicas * capacity

    def kernel(experts_ref, gates_ref, grad_ref, out_ref, target_ref):
        ids = experts_ref[...]
        gate = gates_ref[...]
        expert = lax.broadcasted_iota(jnp.int32, (EXPERT_COUNT, tokens), 0)
        named = [
            jnp.where(ids[k : k + 1] == expert, 1.0, 0.0) for k in range(choices)
        ]
        row = lax.broadcasted_iota(jnp.int32, (tokens, tokens), 0)
        col = lax.broadcasted_iota(jnp.int32, (tokens, tokens), 1)
        upper = jnp.where(row < col, 1.0, 0.0).astype(BF)
        earlier = dot(sum(named).astype(BF), upper)
        place = lax.broadcasted_iota(jnp.int32, (rows, tokens), 0).astype(F32)
        block = jnp.floor((place + 0.5) * (1.0 / capacity))
        owner = jnp.floor((place + 0.5) * (1.0 / (replicas * capacity)))
        slot_row = (place + capacity * (owner - block)).astype(jnp.int32)
        picked = jnp.zeros((rows, tokens), F32)
        weight = jnp.zeros((rows, tokens), F32)
        targets = []
        for k in range(choices):
            slot = jnp.sum(earlier * named[k], axis=0, keepdims=True).astype(jnp.int32)
            target = ids[k : k + 1] * capacity + slot
            match = jnp.where(target == slot_row, 1.0, 0.0)
            picked = picked + match
            weight = weight + match * gate[k : k + 1]
            earlier = earlier + named[k]
            targets.append(target)
        values = dot(picked.astype(BF), grad_ref[...])
        out_ref[...] = (values * jnp.sum(weight, axis=1, keepdims=True)).astype(BF)
        choice = lax.broadcasted_iota(jnp.int32, (choices, tokens), 0)
        chosen = jnp.broadcast_to(targets[0], (choices, tokens))
        for k in range(1, choices):
            chosen = jnp.where(choice == k, targets[k], chosen)
        target_ref[...] = chosen

    out = (
        jax.ShapeDtypeStruct((rows, columns), BF),
        jax.ShapeDtypeStruct((choices, tokens), jnp.int32),
    )
    return whole(kernel, out, experts, gates, output_gradient)


def build_parcel(frozen, d_mixed, up_map, d_rows, totals):
    height, columns = frozen.shape
    devices = totals.shape[0]
    rank = up_map.shape[0]
    peers = d_mixed.shape[0]
    rest = height - LANES

    def kernel(frozen_ref, mixed_ref, up_ref, rows_ref, totals_ref, out_ref):
        flat = mixed_ref[...].reshape(peers * TILE, LANES)
        first = dot(rider_rows(peers, ROWS), flat, ((0,), (0,)))
        second = dot(rider_rows(peers, ROWS + 1), flat, ((0,), (0,)))
        adapter = jnp.concatenate([first, second[:, :rest]], axis=1).astype(BF)
        replicas = devices // EXPERT_COUNT
        share = rank // replicas
        slots = frozen_ref[...] + (LOWRANK_SCALE / replicas) * dot(
            adapter, up_ref[...], ((0,), (0,))
        )
        row = lax.broadcasted_iota(jnp.int32, (share, rank), 0)
        col = lax.broadcasted_iota(jnp.int32, (share, rank), 1)
        chosen = jnp.where(col == row + lax.axis_index("r") * share, 1.0, 0.0).astype(BF)
        part = dot(chosen, adapter).astype(BF)
        up = (LOWRANK_SCALE * dot(part, rows_ref[...])).astype(BF)
        out_ref[:, :share, :] = jnp.broadcast_to(up[None], (devices, share, columns))
        rows = dot(placement(devices, ROWS), slots.astype(BF))
        rows += dot(rider_rows(devices, ROWS), totals_ref[...])
        rows = rows.reshape(devices, TILE, columns)[:, : ROWS + 1]
        out_ref[:, share:, :] = rows.astype(BF)

    share = rank * EXPERT_COUNT // devices
    out = jax.ShapeDtypeStruct((devices, share + ROWS + 1, columns), BF)
    return whole(kernel, out, frozen, d_mixed, up_map, d_rows, totals)


def open_parcel(parcel, experts, gates, target, rank):
    devices, height, columns = parcel.shape
    choices, tokens = experts.shape
    replicas = devices // EXPERT_COUNT
    share = rank // replicas

    def kernel(parcel_ref, experts_ref, gates_ref, target_ref, mixed_ref, up_ref, grad_ref):
        values = parcel_ref[...].astype(F32)
        up_ref[...] = values[:, :share].reshape(EXPERT_COUNT, rank, columns)
        rest = values[:, share:].reshape(EXPERT_COUNT, replicas, ROWS + 1, columns).sum(axis=1)
        gate = gates_ref[...]
        target = target_ref[...]
        slot = target - experts_ref[...] * ROWS
        c = lax.broadcasted_iota(jnp.int32, (ROWS + 1, tokens), 0)
        mixed = jnp.zeros((tokens, columns), F32)
        for e in range(EXPERT_COUNT):
            mixer = jnp.zeros((ROWS + 1, tokens), F32)
            for k in range(choices):
                hit = (target[k : k + 1] == e * ROWS + c) & (c < ROWS)
                mixer = mixer + jnp.where(hit, gate[k : k + 1], 0.0)
            mixed = mixed + lax.dot_general(
                mixer,
                rest[e],
                (((0,), (0,)), ((), ())),
                precision=HIGH_ACCURACY,
                preferred_element_type=F32,
            )
        mixed_ref[...] = mixed.astype(BF)
        totals = jnp.concatenate(
            [rest[e, ROWS : ROWS + 1, :LANES] for e in range(EXPERT_COUNT)], axis=0
        )
        totals = (totals * (1.0 / replicas)).astype(BF)
        expert = lax.broadcasted_iota(jnp.int32, (EXPERT_COUNT, tokens), 0)
        lane = lax.broadcasted_iota(jnp.int32, (LANES, tokens), 0)
        grads = []
        for k in range(choices):
            named = jnp.where(experts_ref[k : k + 1, :] == expert, 1.0, 0.0).astype(BF)
            by_lane = dot(totals, named, ((0,), (0,)))
            at = slot[k : k + 1]
            hit = (lane == at) | (lane == at + ROWS)
            grads.append(jnp.sum(jnp.where(hit, by_lane, 0.0), axis=0, keepdims=True))
        grad_ref[...] = jnp.concatenate(grads, axis=0) / gate

    out = (
        jax.ShapeDtypeStruct((tokens, columns), BF),
        jax.ShapeDtypeStruct((EXPERT_COUNT, rank, columns), F32),
        jax.ShapeDtypeStruct((choices, tokens), F32),
    )
    return whole(kernel, out, parcel, experts, gates, target)


def dequantize(codes, scales, depth, columns):
    stride, width = codes.shape
    groups = scales.shape[0]
    size = stride // groups

    def kernel(codes_ref, scales_ref, all_ref, own_ref, other_ref):
        first = lax.axis_index("c") == 0
        for group in range(groups):
            rows = slice(group * size, (group + 1) * size)
            values = codes_ref[rows, :].astype(F32) * scales_ref[group : group + 1, :]
            all_ref[rows, :] = values.astype(BF)
            low, high = values[:, :columns], values[:, columns:]
            own_ref[0, rows, :] = jnp.where(first, low, high).astype(BF)
            other_ref[0, rows, :] = jnp.where(first, high, low).astype(BF)

    half = pl.BlockSpec((1, stride, columns), lambda z: (z, 0, 0))
    halves = jax.ShapeDtypeStruct((depth, stride, columns), BF)
    return pl.pallas_call(
        kernel,
        grid=(depth,),
        in_specs=[
            pl.BlockSpec((stride, 2 * columns), lambda z: (0, z)),
            pl.BlockSpec((groups, 2 * columns), lambda z: (0, z)),
        ],
        out_specs=(pl.BlockSpec((stride, 2 * columns), lambda z: (0, z)), half, half),
        out_shape=(jax.ShapeDtypeStruct((stride, width), BF), halves, halves),
        cost_estimate=pl.CostEstimate(
            flops=2 * stride * width, bytes_accessed=6 * stride * width, transcendentals=0
        ),
        compiler_params=pltpu.CompilerParams(vmem_limit_bytes=32 * 1024 * 1024),
    )(codes, scales)


def pair_products(rotated, neighbour, own, other):
    depth, stride, columns = own.shape
    height = rotated.shape[0]
    step = 2

    def kernel(rotated_ref, neighbour_ref, own_ref, other_ref, out_ref):
        for z in range(step):
            total = dot(rotated_ref[...], own_ref[z]) + dot(neighbour_ref[...], other_ref[z])
            out_ref[z] = total.astype(BF)

    rows = pl.BlockSpec((height, stride), lambda z: (0, 0))
    half = pl.BlockSpec((step, stride, columns), lambda z: (z, 0, 0))
    return pl.pallas_call(
        kernel,
        grid=(depth // step,),
        in_specs=[rows, rows, half, half],
        out_specs=pl.BlockSpec((step, height, columns), lambda z: (z, 0, 0)),
        out_shape=jax.ShapeDtypeStruct((depth, height, columns), BF),
        cost_estimate=pl.CostEstimate(
            flops=4 * height * stride * depth * columns,
            bytes_accessed=4 * depth * columns * (stride + height),
            transcendentals=0,
        ),
        compiler_params=pltpu.CompilerParams(vmem_limit_bytes=32 * 1024 * 1024),
    )(rotated, neighbour, own, other)


def to_chunks(values, signs):
    height, stride = values.shape
    halves = stride // LANES
    blocks = height // ROWS

    def kernel(values_ref, signs_ref, out_ref):
        sign = (2 * signs_ref[...] - 1).astype(F32)
        signed = (values_ref[...].astype(F32) * sign).astype(BF)
        place = placement(blocks, ROWS)
        for half in range(halves):
            part = dot(place, signed[:, half * LANES : (half + 1) * LANES])
            part = part.astype(BF).reshape(blocks, TILE, LANES)
            out_ref[half * blocks : (half + 1) * blocks] = part

    out = jax.ShapeDtypeStruct((halves * blocks, TILE, LANES), BF)
    return whole(kernel, out, values, signs.reshape(1, stride))


def hadamard(parts):
    step = 1
    while step < len(parts):
        for low in range(len(parts)):
            if low & step == 0:
                one, two = parts[low], parts[low + step]
                parts[low], parts[low + step] = one + two, one - two
        step *= 2
    return parts


def mix_blocks(chunks):
    def kernel(chunks_ref, out_ref, sum_ref):
        values = chunks_ref[...].astype(F32)
        mixed = hadamard([values[p] for p in range(values.shape[0])])
        row = lax.broadcasted_iota(jnp.int32, (TILE, LANES), 0)
        sum_ref[...] = mixed[0]
        for p, part in enumerate(mixed):
            out_ref[p] = jnp.where(row < ROWS, part, mixed[0]).astype(BF)

    out = jax.ShapeDtypeStruct(chunks.shape, BF), jax.ShapeDtypeStruct((TILE, LANES), F32)
    return whole(kernel, out, chunks)


def gather_rows(chunks, blocks):
    flat = chunks.reshape(-1, LANES)
    place = placement(blocks, ROWS)
    size = blocks * TILE
    halves = flat.shape[0] // size
    parts = [
        dot(place, flat[half * size : (half + 1) * size], ((0,), (0,))) for half in range(halves)
    ]
    return jnp.concatenate(parts, axis=1)


def finish_rotation(chunks, spread, scaling):
    blocks = chunks.shape[0] * LANES // spread.shape[0]

    def kernel(chunks_ref, spread_ref, out_ref):
        values = gather_rows(chunks_ref[...], blocks).astype(BF)
        out_ref[...] = (dot(values, spread_ref[...]) * scaling).astype(BF)

    out = jax.ShapeDtypeStruct((blocks * ROWS, spread.shape[0]), BF)
    return whole(kernel, out, chunks, spread)


def finish_gradient(chunks, signs):
    stride = signs.shape[0]
    blocks = chunks.shape[0] * LANES // stride

    def kernel(chunks_ref, signs_ref, out_ref):
        sign = (2 * signs_ref[...] - 1).astype(F32)
        out_ref[...] = (gather_rows(chunks_ref[...], blocks) * sign).astype(BF)

    out = jax.ShapeDtypeStruct((blocks * ROWS, stride), BF)
    return whole(kernel, out, chunks, signs.reshape(1, stride))


def backward_chunks(main, adapter_grad, down_map, rotated, spread, scaling):
    height, stride = main.shape
    halves = stride // LANES
    blocks = height // ROWS
    peers = halves * blocks
    rest = height - LANES

    def kernel(main_ref, grad_ref, down_ref, rotated_ref, spread_ref, out_ref):
        rotated_value = rotated_ref[...]
        down = down_ref[...]
        d_rotated = main_ref[...] + dot(grad_ref[...], down, ((1,), (1,)))
        local = dot(d_rotated.astype(BF), spread_ref[...])
        local = (local * scaling).astype(BF)
        product = rotated_value.astype(F32) * d_rotated
        totals = lax.dot_general(
            jnp.ones((TILE, stride), F32),
            product,
            (((1,), (1,)), ((), ())),
            precision=HIGH_ACCURACY,
            preferred_element_type=F32,
        )
        adapter = dot(down, rotated_value, ((0,), (1,))).astype(BF)
        pad = jnp.zeros((peers, LANES - rest), BF)
        riders = dot(rider_rows(peers, ROWS), adapter[:, :LANES])
        tail = jnp.concatenate([adapter[:, LANES:], pad], axis=1)
        riders += dot(rider_rows(peers, ROWS + 1), tail)
        row_tail = jnp.concatenate(
            [totals[:, LANES:], jnp.zeros((TILE, LANES - rest), F32)], axis=1
        )
        row_tail = pltpu.roll(row_tail, rest, 1)
        k = lax.broadcasted_iota(jnp.int32, (TILE, LANES), 0)
        extra = jnp.where(k == ROWS + 2, totals[:, :LANES], 0.0)
        extra += jnp.where(k == ROWS + 1, row_tail, 0.0)
        place = placement(blocks, ROWS)
        for half in range(halves):
            part = dot(place, local[:, half * LANES : (half + 1) * LANES])
            part += riders[half * blocks * TILE : (half + 1) * blocks * TILE]
            part = part.reshape(blocks, TILE, LANES) + extra[None]
            out_ref[half * blocks : (half + 1) * blocks] = part.astype(BF)

    out = jax.ShapeDtypeStruct((peers, TILE, LANES), BF)
    return whole(kernel, out, main, adapter_grad, down_map, rotated, spread)


def split(values):
    high = lax.reduce_precision(values, 8, 7)
    return high, lax.reduce_precision(values - high, 8, 7)


def body(
    hidden, codes, scales, signs, lowrank_down_map, lowrank_up_map, experts, gates, output_gradient
):
    slot_rows, stride = hidden.shape
    replicas, depth = lax.axis_size("r"), lax.axis_size("z")
    devices = EXPERT_COUNT * replicas
    rank = lowrank_down_map.shape[1]
    expert_position = lax.axis_index("e")
    capacity = slot_rows // devices
    columns = output_gradient.shape[1]
    scaling = 1.0 / math.sqrt(HIDDEN_UNITS)

    lowrank_local = lax.dynamic_index_in_dim(lowrank_up_map, expert_position, 0, keepdims=False)
    padded = jnp.pad(lowrank_local, ((0, rank // 2), (0, 0)))
    lowrank_full = lax.all_gather(padded, TENSOR, axis=1, tiled=True)[:rank]
    outgoing, target = route(experts.T, gates.T, output_gradient, replicas, capacity)
    weights, own, other = dequantize(codes, scales, depth, columns)
    d_rows = exchange(outgoing, EXPERT)
    chunks = to_chunks(hidden, signs)
    d_rows, weights, own, other, chunks = lax.optimization_barrier(
        (d_rows, weights, own, other, chunks)
    )
    d_full = lax.all_gather(d_rows, TENSOR, axis=1, tiled=True)

    spread_local = sylvester(stride)
    mixed_blocks, _ = mix_blocks(exchange(chunks, SLAB))
    rotated = finish_rotation(exchange(mixed_blocks, SLAB), spread_local, scaling)

    other = lax.ppermute(other, "c", [(0, 1), (1, 0)])
    neighbour = lax.ppermute(rotated, "c", [(0, 1), (1, 0)])
    pair = pair_products(rotated, neighbour, own, other)
    frozen = lax.psum_scatter(pair, "z", scatter_dimension=0, tiled=False).astype(F32)

    adapter_grad = LOWRANK_SCALE * lax.dot_general(
        d_full, lowrank_full, (((1,), (1,)), ((), ())), preferred_element_type=F32
    )
    adapter_grad = adapter_grad.astype(BF)
    main = dot(d_full, weights, ((1,), (1,)))
    down_map_gradient = dot(rotated, adapter_grad, ((0,), (0,)))
    d_chunks = exchange(
        backward_chunks(main, adapter_grad, lowrank_down_map, rotated, spread_local, scaling), SLAB
    )
    d_mixed, sums = mix_blocks(d_chunks)
    rest = slot_rows - LANES
    row_total = jnp.concatenate([sums[ROWS + 2], sums[ROWS + 1, rest : 2 * rest]])
    d_mixed = exchange(d_mixed, SLAB)
    hidden_gradient = finish_gradient(d_mixed, signs)

    totals = jnp.concatenate(
        [part.astype(BF).reshape(devices, capacity) for part in split(row_total)], axis=1
    )
    totals = jnp.pad(totals, ((0, 0), (0, columns - 2 * capacity)))
    parcel = exchange(build_parcel(frozen, d_mixed, lowrank_local, d_rows, totals), EXPERT)
    mixed, up_map_gradient, gates_gradient = open_parcel(
        parcel, experts.T, gates.T, target, rank
    )
    return (mixed, hidden_gradient, down_map_gradient, up_map_gradient, gates_gradient.T)


def solution(mesh):
    owners, tensor = mesh.devices.shape
    split = Mesh(
        mesh.devices.reshape(EXPERT_COUNT, owners // EXPERT_COUNT, tensor // 2, 2),
        ("e", "r", "z", "c"),
    )
    every = EXPERT + TENSOR
    placed = (
        P(None, every),
        P(every, None),
        P(every, None),
        P(every),
        P(every, None),
        P(None, None, TENSOR),
        P(EXPERT, None),
        P(EXPERT, None),
        P(EXPERT, TENSOR),
    )
    return jax.shard_map(
        body,
        mesh=split,
        in_specs=placed,
        out_specs=(
            P(EXPERT, TENSOR),
            P(None, every),
            P(every, None),
            P(None, None, TENSOR),
            P(EXPERT, None),
        ),
        check_vma=False,
    )
```
